512 devices in a mesh: tm: 64 (over z_lo, y, core), dp: 8 (over x, z_hi).
Axes of the slice: x: 4, y: 4, z: 16 (z_hi: 2, z_lo: 8; z = z_hi * 8 + z_lo), core: 2. Of those that a mesh axis runs over, the one named last changes fastest.
Arguments:
- latent: bfloat16 [8, 128, 4, 8, 384], P('dp', 'tm'), may hold values from -6 to 6
- frame_pos: int32 [8, 128], P('dp', 'tm'), may hold values from 0 to 127, as said below
- w_short: bfloat16 [384, 192], replicated, may hold values from -0.3125 to 0.3125
- gain: float32 [192], replicated, may hold values from 0.1 to 1.9
- w_conv: bfloat16 [3, 3, 3, 192, 192], replicated, may hold values from -0.078125 to 0.078125
- cotangent: bfloat16 [8, 128, 8, 16, 192], P('dp', 'tm'), may hold values from -16 to 16
Outputs:
- decoded: bfloat16 [8, 128, 8, 16, 192], P('dp', 'tm')
- grad_latent: bfloat16 [8, 128, 4, 8, 384], P('dp', 'tm')
- grad_conv: float32 [192, 5184], P('dp')
- grad_short: float32 [384, 192], replicated
- grad_gain: float32 [192], replicated
The draws below stay inside these ranges and needn't reach their ends.
Inputs may be any that keep to these rules, and one draw needn't show every extreme that they name: frame_pos is 0 at the first frame of a clip and rises by one per frame within a clip; the first frame of every group starts a clip.
All inputs are finite; a program needn't handle non-finite values.
Results may differ from the reference program's by a relative error of at most 0.015.
Values may be sent and summed in bfloat16 or wider, within the bound.
No kernel may reach another device: no remote copies, remote signals or barrier semaphores. Data moves between devices by JAX's collectives and lax.ppermute only.
A program may use at most 64 MiB of HBM per device.

```python
import jax
import jax.numpy as jnp
from jax import lax

C_IN = 384
C = 192
H = 4
W = 8
GROUPS = 8
FRAMES_G = 128
HO = 8
WO = 16


def draw_frame_pos(key, part):
    key = jax.random.fold_in(key, 7)
    starts = jax.random.randint(key, (GROUPS, FRAMES_G), 0, 48) == 0
    index = jnp.arange(FRAMES_G, dtype=jnp.int32)[None, :]
    group_index = jnp.arange(GROUPS, dtype=jnp.int32)[:, None]
    starts = starts & (group_index != 0) | (index == 0)
    begin = lax.cummax(jnp.where(starts, index, 0).astype(jnp.int32), axis=1)
    return (index - begin).astype(jnp.int32)


def raised(result, key, source, target, parts, factor):
    owner, partner = [(jnp.arange(result.shape[dim]) // (result.shape[dim] // parts)).reshape([-1 if axis == dim else 1 for axis in range(result.ndim)]) for dim in (source, target)]
    chosen = jax.random.permutation(key, parts)[partner]
    strong = (owner == chosen) | (owner == (partner + parts // 2) % parts)
    return jnp.where(strong, factor * result, result)


def block_scale(key, dims, split, smallest, largest):
    loudness, own = 1.0, jax.random.fold_in(key, 6)
    for position, blocks in split:
        draws = jnp.exp(jax.random.uniform(jax.random.fold_in(own, position), (blocks,), jnp.float32, smallest / len(split), largest / len(split)))
        loudness = loudness * jnp.repeat(draws, dims[position] // blocks).reshape([-1 if axis == position else 1 for axis in range(len(dims))])
    return loudness


def normal_values(key, shape, scale, bound, cuts=(), kind=jnp.bfloat16):
    level = block_scale(key, shape, cuts, -0.22, 0.18) if cuts else 1.0
    values = jax.random.normal(key, shape, jnp.float32) * scale * level
    return jnp.minimum(jnp.maximum(values, -bound), bound).astype(kind)


def gaussian_with(stream_key, dims, scale, bound, cuts, heavy, kind=jnp.bfloat16):
    drawn = scale * jax.random.normal(stream_key, dims, jnp.float32)
    if cuts:
        drawn = drawn * block_scale(stream_key, dims, cuts, -0.22, 0.18)
    return jnp.clip(raised(drawn, jax.random.fold_in(stream_key, 3), *heavy), -bound, bound).astype(kind)


def setup_inputs(seed: int = 0) -> dict:
    arg_keys = jax.random.split(jax.random.key(seed), 7)
    return {
        "latent": normal_values(arg_keys[0], (GROUPS, FRAMES_G, H, W, C_IN), 1.0, 6.0, ((0, 8), (1, 64))),
        "frame_pos": draw_frame_pos(jax.random.fold_in(arg_keys[6], 71), 0),
        "w_short": normal_values(arg_keys[2], (C_IN, C), C_IN ** -0.5, 0.3125),
        "gain": jnp.clip(1.0 + 0.18 * jax.random.normal(arg_keys[3], (C,), jnp.float32), 0.1, 1.9),
        "w_conv": normal_values(arg_keys[4], (3, 3, 3, C, C), (27 * C) ** -0.5, 0.078125),
        "cotangent": gaussian_with(arg_keys[5], (GROUPS, FRAMES_G, HO, WO, C), 1.0, 16.0, ((0, 8), (1, 64)), (1, 4, 64, 4.0)),
    }


EPS = 1e-06

def enlarge(value):
    return jnp.repeat(jnp.repeat(value, 2, axis=1), 2, axis=2)

def pool_sum(value):
    frames, rows, cols, width = value.shape
    return value.reshape(frames, rows // 2, 2, cols // 2, 2, width).sum(axis=(2, 4))

def plane_conv(inputs, kernel):
    return lax.conv_general_dilated(inputs, kernel, (1, 1), ((1, 1), (1, 1)), dimension_numbers=('NHWC', 'HWIO', 'NHWC'), preferred_element_type=jnp.float32)

def adjoint_conv(grad, kernel):
    return plane_conv(grad, jnp.transpose(kernel[::-1, ::-1], (0, 1, 3, 2)))

def patches_of(frames):
    rows, cols = (frames.shape[1], frames.shape[2])
    padded = jnp.pad(frames, ((0, 0), (1, 1), (1, 1), (0, 0)))
    return jnp.concatenate([padded[:, a:a + rows, b:b + cols, :] for a in range(3) for b in range(3)], axis=-1)

def reference(latent, frame_pos, w_short, gain, w_conv, cotangent):
    c_in, width = w_short.shape
    decoded_all = []
    latent_all = []
    grad_conv = jnp.zeros((width, 27 * width), jnp.float32)
    grad_short = jnp.zeros((c_in, width), jnp.float32)
    grad_gain = jnp.zeros((width,), jnp.float32)
    for group in range(GROUPS):
        inputs = latent[group]
        pos = frame_pos[group]
        grad_out = cotangent[group]
        frames, rows, cols = (inputs.shape[0], inputs.shape[1], inputs.shape[2])
        s_val = jnp.dot(inputs.reshape(-1, c_in), w_short, preferred_element_type=jnp.float32).reshape(frames, rows, cols, width)
        scale = lax.rsqrt(lax.optimization_barrier(jnp.mean(s_val * s_val, axis=-1, keepdims=True)) + EPS)
        normed = s_val * scale
        z_val = normed * gain
        sig = jax.nn.sigmoid(z_val)
        act = (z_val * sig).astype(jnp.bfloat16)
        extended = enlarge(jnp.concatenate([jnp.zeros((2, rows, cols, width), jnp.bfloat16), act], axis=0))
        masks = [(pos >= 2 - k)[:, None, None, None] for k in range(3)]
        output = enlarge(s_val)
        for k in range(3):
            output = output + jnp.where(masks[k], plane_conv(extended[k:k + frames], w_conv[k]), 0.0)
        decoded_all.append(output.astype(jnp.bfloat16))
        grad_up = jnp.zeros((frames + 2, 2 * rows, 2 * cols, width), jnp.float32)
        pieces = []
        for k in range(3):
            masked = grad_out * masks[k].astype(jnp.bfloat16)
            grad_up = grad_up.at[k:k + frames].add(adjoint_conv(masked, w_conv[k]))
            pieces.append(patches_of(extended[k:k + frames]) * masks[k].astype(jnp.bfloat16))
        table = jnp.concatenate(pieces, axis=-1).reshape(-1, 27 * width)
        grad_conv = grad_conv + lax.dot_general(grad_out.reshape(-1, width), table, (((0,), (0,)), ((), ())), preferred_element_type=jnp.float32)
        grad_act = pool_sum(grad_up[2:])
        dz_val = grad_act * sig * (1.0 + z_val * (1.0 - sig))
        grad_gain = grad_gain + lax.optimization_barrier(jnp.sum(dz_val * normed, axis=(0, 1, 2)))
        dn_val = dz_val * gain
        ds_val = scale * (dn_val - normed * lax.optimization_barrier(jnp.mean(dn_val * normed, axis=-1, keepdims=True))) + pool_sum(grad_out.astype(jnp.float32))
        ds_flat = ds_val.astype(jnp.bfloat16).reshape(-1, width)
        latent_all.append(lax.dot_general(ds_flat, w_short, (((1,), (1,)), ((), ())), preferred_element_type=jnp.float32).astype(jnp.bfloat16).reshape(inputs.shape))
        grad_short = grad_short + lax.dot_general(inputs.reshape(-1, c_in), ds_flat, (((0,), (0,)), ((), ())), preferred_element_type=jnp.float32)
    return (jnp.stack(decoded_all), jnp.stack(latent_all), grad_conv, grad_short, grad_gain)
```

```python
import functools

import jax
import jax.numpy as jnp
import numpy as np
from jax import lax
from jax.experimental import pallas as pl
from jax.experimental.pallas import tpu as pltpu
from jax.sharding import Mesh, PartitionSpec as P

EPS = 1e-06
C_IN = 384
C = 192
CELLS = 32
FINE = 128
TAPS = 27
CONV_ROWS = 256
SHORT_ROWS = 80
MSG = CONV_ROWS + SHORT_ROWS
BF16 = jnp.bfloat16
F32 = jnp.float32


def pool_matrix(frames):
    out = np.zeros((frames, 8, 16, 3, 3, frames, 4, 8), np.float32)
    for t in range(frames):
        for a in range(3):
            for b in range(3):
                for p in range(8):
                    for q in range(16):
                        row, col = p + a - 1, q + b - 1
                        if 0 <= row < 8 and 0 <= col < 16:
                            out[t, p, q, a, b, t, row // 2, col // 2] = 1
    return out.reshape(frames * FINE, 9 * frames * CELLS)


def dot(a, b):
    return jnp.dot(a, b, preferred_element_type=F32)


def features(inputs, w_short, gain):
    s_val = dot(inputs, w_short)
    scale = lax.rsqrt(jnp.mean(s_val * s_val, axis=-1, keepdims=True) + EPS)
    normed = s_val * scale
    z_val = normed * gain
    sig = 1.0 / (1.0 + jnp.exp(-z_val))
    return s_val, scale, normed, z_val, sig, (z_val * sig).astype(BF16)


def grad_kernel(
    core_ref, pos_ref, lat_ref, w_short_ref, gain_ref, cot_ref, next_ref, w_conv_ref, pool_ref,
    keep_ref, send_ref, s_ref, act_ref, ds_ref,
    msg, ct, sems,
):
    lat = lat_ref[...]
    gain = gain_ref[...]
    s_val, scale, normed, z_val, sig, act = features(lat, w_short_ref[...], gain)
    s_ref[...] = s_val
    act_ref[...] = act
    follows = (pos_ref[1] >= 1).astype(F32)

    fine = jnp.concatenate([cot_ref[...], next_ref[...]], axis=0)
    fine_t = jnp.transpose(fine)
    pooled = None
    for ab in range(9):
        part = dot(fine_t, pool_ref[:, ab * 128 : (ab + 1) * 128])
        if ab == 4:
            pooled = jnp.transpose(part)[: 2 * CELLS]
        ct[ab] = part.astype(BF16)

    turned = []
    for k in range(3):
        acc = dot(w_conv_ref[9 * k], ct[0])
        for ab in range(1, 9):
            acc = acc + dot(w_conv_ref[9 * k + ab], ct[ab])
        turned.append(jnp.transpose(acc))
    early = turned[2][:32] + follows * (turned[1][32:64] + turned[0][64:96])
    late = turned[2][32:64] + turned[1][64:96] + turned[0][96:]
    grad_act = jnp.concatenate([early, late], axis=0)
    dz_val = grad_act * sig * (1.0 + z_val * (1.0 - sig))
    gain_term = jnp.sum(dz_val * normed, axis=0, keepdims=True)
    dn_val = dz_val * gain
    ds_val = scale * (dn_val - normed * jnp.mean(dn_val * normed, axis=-1, keepdims=True)) + pooled
    ds_flat = ds_val.astype(BF16)
    ds_ref[...] = ds_flat

    act0 = (act[:CELLS].astype(F32) * follows).astype(BF16)
    act1 = act[CELLS:]
    none = jnp.zeros((CELLS, C), BF16)
    rows = [[none, none, act0, act1], [none, act0, act1, none], [act[:CELLS], act1, none, none]]
    gap = jnp.zeros((4 * CELLS, 64), BF16)
    stacked = [jnp.concatenate(r, axis=0) for r in rows]
    first = [jnp.concatenate([v, gap], axis=1) for v in stacked]
    second = [jnp.concatenate([gap, v], axis=1) for v in stacked]

    def place(tile_pair, index):
        for d in range(8):
            x, zh = d // 2, d % 2
            block = jnp.concatenate([t[24 * d : 24 * d + 24] for t in tile_pair], axis=0).astype(BF16)
            for i in range(3):
                q = 3 * index + i
                c, y, zl = q // 32, (q // 8) % 4, q % 8
                row = zh * 128 + zl * 16
                msg[c, 4 * x + y, row : row + 16] = block[16 * i : 16 * i + 16]

    waiting = []
    index = 0
    for n in range(0, TAPS, 2):
        even = dot(ct[n % 9], first[n // 9])
        waiting.append(even[:, :128])
        if n + 1 < TAPS:
            odd = dot(ct[(n + 1) % 9], second[(n + 1) // 9])
            waiting.append(even[:, 128:] + odd[:, :128])
            waiting.append(odd[:, 128:])
        else:
            waiting.append(even[:, 128:])
        while len(waiting) >= 2:
            place(waiting[:2], index)
            waiting = waiting[2:]
            index += 1
    place([waiting[0], jnp.zeros((C, 128), F32)], index)
    for d in range(8):
        x, zh = d // 2, d % 2
        row = zh * 128 + 7 * 16
        msg[1, 4 * x + 3, row : row + 16] = jnp.zeros((16, 128), BF16)

    short = dot(jnp.transpose(lat), ds_flat)
    tail = jnp.concatenate([short[:192, 128:], short[192:, 128:]], axis=1)
    last = jnp.concatenate(
        [gain_term[:, :128], jnp.concatenate([gain_term[:, 128:], jnp.zeros((1, 64), F32)], axis=1),
         jnp.zeros((14, 128), F32)], axis=0)
    flat = jnp.concatenate([short[:, :128], tail, last, jnp.zeros((48, 128), F32)], axis=0).astype(BF16)
    for i in range(40):
        c, y, z5 = i // 20, (i // 5) % 4, i % 5
        row = CONV_ROWS + 16 * z5
        for x in range(4):
            msg[c, 4 * x + y, row : row + 16] = flat[16 * i : 16 * i + 16]

    core = core_ref[0]
    out = pltpu.make_async_copy(msg.at[1 - core], send_ref, sems.at[0])
    own = pltpu.make_async_copy(msg.at[core], keep_ref, sems.at[1])
    out.start()
    own.start()
    out.wait()
    own.wait()


def forward_kernel(
    pos_ref, before_ref, w_short_ref, gain_ref, s_ref, act_ref, ds_ref, w_conv_ref, spread_ref,
    decoded_ref, grad_latent_ref, z_all,
):
    w_short = w_short_ref[...]
    grad_latent_ref[...] = lax.dot_general(
        ds_ref[...], w_short, (((1,), (1,)), ((), ())), preferred_element_type=F32
    ).astype(BF16)
    prev = features(before_ref[...], w_short, gain_ref[...])[-1].astype(F32)
    act = act_ref[...]
    valid = [[(pos_ref[t] >= 2 - k).astype(F32) for k in range(2)] for t in range(2)]
    taps = [
        jnp.concatenate([prev[:CELLS] * valid[0][0], prev[CELLS:] * valid[1][0]], axis=0).astype(BF16),
        jnp.concatenate([prev[CELLS:] * valid[0][1], act[:CELLS].astype(F32) * valid[1][1]], axis=0).astype(BF16),
        act,
    ]
    for ab in range(9):
        acc = dot(taps[0], w_conv_ref[ab]) + dot(taps[1], w_conv_ref[9 + ab]) + dot(taps[2], w_conv_ref[18 + ab])
        if ab == 4:
            acc = acc + s_ref[...]
        z_all[64 * ab : 64 * ab + 64] = acc.astype(BF16)
    decoded_ref[...] = dot(spread_ref[...], z_all[...]).astype(BF16)


def shape(*dims, dtype=BF16):
    return jax.ShapeDtypeStruct(dims, dtype)


def on_device(latent, frame_pos, w_short, gain, w_conv, cotangent):
    pos = frame_pos[0]
    lat = latent.reshape(2 * CELLS, C_IN)
    cot = cotangent.reshape(2 * FINE, C)
    gain2 = gain.reshape(1, C)
    w27 = w_conv.reshape(TAPS, C, C)
    smem = pl.BlockSpec(memory_space=pltpu.SMEM)
    vmem = pl.BlockSpec(memory_space=pltpu.VMEM)
    any_space = pl.BlockSpec(memory_space=pl.ANY)
    params = pltpu.CompilerParams(vmem_limit_bytes=40 * 1024 * 1024)

    tm = ("zl", "y", "c")
    keep0 = (pos[0] >= 1).astype(BF16)
    keep1 = (pos[1] >= 2).astype(BF16)
    weight = jnp.concatenate([jnp.full((FINE, 1), keep0), jnp.full((FINE, 1), keep1)], axis=0)
    following = lax.ppermute(cot * weight, tm, [(i + 1, i) for i in range(63)])
    before = lax.ppermute(lat, tm, [(i, i + 1) for i in range(63)])

    pool = jnp.asarray(pool_matrix(4), BF16)
    spread = jnp.asarray(pool_matrix(2), BF16)
    core = lax.axis_index("c").astype(jnp.int32).reshape(1)
    keep, send, s_val, act, ds_flat = pl.pallas_call(
        grad_kernel,
        out_shape=[
            shape(16, MSG, 128), shape(16, MSG, 128), shape(2 * CELLS, C, dtype=F32),
            shape(2 * CELLS, C), shape(2 * CELLS, C),
        ],
        in_specs=[smem, smem] + [vmem] * 7,
        out_specs=[any_space, any_space, vmem, vmem, vmem],
        scratch_shapes=[
            pltpu.VMEM((2, 16, MSG, 128), BF16),
            pltpu.VMEM((9, C, 128), BF16),
            pltpu.SemaphoreType.DMA((2,)),
        ],
        compiler_params=params,
        name="grad_kernel",
    )(core, pos, lat, w_short, gain2, cot, following, w27, pool)

    other = lax.ppermute(send, "c", [(0, 1), (1, 0)])
    decoded, grad_latent = pl.pallas_call(
        forward_kernel,
        out_shape=[shape(2 * FINE, C), shape(2 * CELLS, C_IN)],
        in_specs=[smem] + [vmem] * 8,
        out_specs=[vmem, vmem],
        scratch_shapes=[pltpu.VMEM((9 * 2 * CELLS, C), BF16)],
        compiler_params=params,
        name="forward_kernel",
    )(pos, before, w_short, gain2, s_val, act, ds_flat, w27, spread)

    half = (keep.astype(F32) + other.astype(F32)).astype(BF16)
    got = lax.all_to_all(half, ("x", "y"), 0, 0)
    part = jnp.sum(got.astype(F32), axis=0).astype(BF16)
    conv = part[:CONV_ROWS].reshape(2, 8, 16, 128)
    rest = jnp.pad(part[CONV_ROWS:].reshape(5, 16, 128), ((0, 3), (0, 0), (0, 0)))
    both = jnp.concatenate([conv, jnp.broadcast_to(rest, (2, 8, 16, 128))], axis=2).reshape(16, 32, 128)
    got = lax.all_to_all(both, ("zh", "zl"), 0, 0)
    whole = jnp.sum(got.astype(F32), axis=0).astype(BF16)
    got = lax.all_to_all(jnp.broadcast_to(whole, (8, 32, 128)), "zl", 0, 0)
    got = lax.all_to_all(jnp.broadcast_to(got, (8, 8, 32, 128)), ("c", "y"), 0, 0)
    flat = got[:, :, :16].reshape(1024, 128)[:984].reshape(41, 24, 128)
    grad_conv = jnp.transpose(flat, (1, 0, 2)).reshape(24, 41 * 128)[:, : TAPS * C].astype(F32)
    small = got[:, :5, 16:].reshape(640, 128).astype(F32)
    grad_short = jnp.concatenate(
        [small[:384], jnp.concatenate([small[384:576, :64], small[384:576, 64:]], axis=0)], axis=1
    )
    grad_gain = small[576:578].reshape(256)[:C]
    return (
        decoded.reshape(cotangent.shape),
        grad_latent.reshape(latent.shape),
        grad_conv,
        grad_short,
        grad_gain,
    )


def solution(mesh):
    fine = Mesh(mesh.devices.reshape(8, 4, 2, 4, 2), ("zl", "y", "c", "x", "zh"))
    tm, dp = ("zl", "y", "c"), ("x", "zh")
    return jax.shard_map(
        on_device,
        mesh=fine,
        in_specs=(
            P(dp, tm, None, None, None),
            P(dp, tm),
            P(),
            P(),
            P(),
            P(dp, tm, None, None, None),
        ),
        out_specs=(
            P(dp, tm, None, None, None),
            P(dp, tm, None, None, None),
            P(dp, None),
            P(),
            P(),
        ),
        check_vma=False,
    )
```

```python
import jax
import jax.numpy as jnp
import numpy as np
from jax import lax
from jax.experimental import pallas as pl
from jax.experimental.pallas import tpu as pltpu
from jax.sharding import Mesh, PartitionSpec as P

EPS = 1e-06
C_IN = 384
C = 192
CELLS = 32
FINE = 128
TAPS = 27
TILES = 41
SHORT_ROWS = 80
SEND_ROWS = 192 + SHORT_ROWS
MSG = 256 + SHORT_ROWS
BF16 = jnp.bfloat16
F32 = jnp.float32


def pool_matrix(frames):
    out = np.zeros((frames, 8, 16, 3, 3, frames, 4, 8), np.float32)
    for t in range(frames):
        for a in range(3):
            for b in range(3):
                for p in range(8):
                    for q in range(16):
                        row, col = p + a - 1, q + b - 1
                        if 0 <= row < 8 and 0 <= col < 16:
                            out[t, p, q, a, b, t, row // 2, col // 2] = 1
    return out.reshape(frames * FINE, 9 * frames * CELLS)


def dot(a, b):
    return jnp.dot(a, b, preferred_element_type=F32)


def dot_nt(a, b):
    return lax.dot_general(a, b, (((1,), (1,)), ((), ())), preferred_element_type=F32)


def features(inputs, w_short_t, gain):
    s_val = dot_nt(inputs, w_short_t)
    scale = lax.rsqrt(jnp.mean(s_val * s_val, axis=-1, keepdims=True) + EPS)
    normed = s_val * scale
    z_val = normed * gain
    sig = 1.0 / (1.0 + jnp.exp(-z_val))
    return s_val, scale, normed, z_val, sig, (z_val * sig).astype(BF16)


def local_kernel(
    next_pos_ref, next_ref, pos_hbm, lat_hbm, w_short_hbm, gain_hbm, cot_hbm, pool_hbm, w_conv_hbm,
    send_ref, s_ref, act_ref, ds_ref,
    pos_ref, lat_ref, w_short_ref, gain_ref, cot_ref, pool_ref, w_conv_ref, turned_ref, ct, sems,
):
    loads = [
        pltpu.make_async_copy(source, target, sems.at[i])
        for i, (source, target) in enumerate([
            (pos_hbm, pos_ref), (lat_hbm, lat_ref), (w_short_hbm, w_short_ref), (gain_hbm, gain_ref),
            (cot_hbm, cot_ref), (pool_hbm, pool_ref), (w_conv_hbm, w_conv_ref),
        ])
    ]
    for load in loads:
        load.start()
    for load in loads[:4]:
        load.wait()
    lat = lat_ref[...]
    gain = gain_ref[...]
    s_val, scale, normed, z_val, sig, act = features(lat, w_short_ref[...], gain)
    s_ref[...] = s_val
    act_ref[...] = act
    follows = (pos_ref[0, 1] >= 1).astype(F32)
    keep0 = (next_pos_ref[0, 0] >= 1).astype(F32)
    keep1 = (next_pos_ref[0, 1] >= 2).astype(F32)

    after = next_ref[...].astype(F32)
    loads[4].wait()
    fine = jnp.concatenate([cot_ref[...].astype(F32), after[:FINE] * keep0, after[FINE:] * keep1], axis=0)
    fine_t = jnp.transpose(fine)
    for tile in range(4):
        turned_ref[tile] = fine_t[:, 128 * tile : 128 * tile + 128]
    for j in range(8):
        parts = []
        for tile in range(4):
            for r in range(3):
                parts.append(turned_ref[tile, pl.ds(8 * r + j, 8, stride=24), :])
        send_ref[j, :96] = jnp.concatenate(parts, axis=0).astype(BF16)
    tail = jnp.concatenate([act[:CELLS, 128:], act[CELLS:, 128:]], axis=1)
    packed = jnp.concatenate([act[:, :128], tail], axis=0)
    for j in range(8):
        send_ref[j, 96:192] = packed

    fine_t = fine_t.astype(BF16)
    loads[5].wait()
    pooled = None
    for ab in range(9):
        part = dot(fine_t, pool_ref[:, ab * 128 : (ab + 1) * 128])
        if ab == 4:
            pooled = jnp.transpose(part)[: 2 * CELLS]
        ct[ab] = part.astype(BF16)

    loads[6].wait()
    turned = []
    for k in range(3):
        acc = dot(w_conv_ref[9 * k], ct[0])
        for ab in range(1, 9):
            acc = acc + dot(w_conv_ref[9 * k + ab], ct[ab])
        turned.append(jnp.transpose(acc))
    early = turned[2][:32] + follows * (turned[1][32:64] + turned[0][64:96])
    late = turned[2][32:64] + turned[1][64:96] + turned[0][96:]
    grad_act = jnp.concatenate([early, late], axis=0)
    dz_val = grad_act * sig * (1.0 + z_val * (1.0 - sig))
    gain_term = jnp.sum(dz_val * normed, axis=0, keepdims=True)
    dn_val = dz_val * gain
    ds_val = scale * (dn_val - normed * jnp.mean(dn_val * normed, axis=-1, keepdims=True)) + pooled
    ds_flat = ds_val.astype(BF16)
    ds_ref[...] = ds_flat

    short_t = dot(jnp.transpose(ds_val).astype(BF16), lat)
    last = jnp.concatenate(
        [gain_term[:, :128], jnp.concatenate([gain_term[:, 128:], jnp.zeros((1, 64), F32)], axis=1),
         jnp.full((1, 128), follows), jnp.zeros((5, 128), F32)], axis=0)
    for j in range(8):
        rows = short_t[24 * j : 24 * j + 24]
        flat = jnp.concatenate([rows[:, :128], rows[:, 128:256], rows[:, 256:], last], axis=0)
        send_ref[j, 192:] = flat.astype(BF16)


def kernel_grad_kernel(got_ref, pool_hbm, out_ref, pool_ref, even_ref, odd_ref, rhs_ref, flat_ref, sem):
    load_pool = pltpu.make_async_copy(pool_hbm, pool_ref, sem)
    load_pool.start()
    none = jnp.zeros((CELLS, C), F32)
    gap = jnp.zeros((4 * CELLS, 64), F32)
    peers = []
    short = jnp.zeros((SHORT_ROWS, 128), F32)
    for p in range(8):
        block = got_ref[p, :96].astype(F32)
        peers.append(jnp.concatenate([block[24 * i : 24 * i + 24] for i in range(4)], axis=1))
        tail = got_ref[p, 160:192].astype(F32)
        act = jnp.concatenate(
            [got_ref[p, 96:160].astype(F32), jnp.concatenate([tail[:, :64], tail[:, 64:]], axis=0)], axis=1)
        extra = got_ref[p, 192:].astype(F32)
        short = short + extra
        act0, act1 = act[:CELLS], act[CELLS:]
        mine = act0 * extra[74:75, :1]
        rows = [[none, none, mine, act1], [none, mine, act1, none], [act0, act1, none, none]]
        for k in range(3):
            value = jnp.concatenate(rows[k], axis=0)
            rhs_ref[2 * k, 128 * p : 128 * p + 128] = jnp.concatenate([value, gap], axis=1).astype(BF16)
            rhs_ref[2 * k + 1, 128 * p : 128 * p + 128] = jnp.concatenate([gap, value], axis=1).astype(BF16)
    fine_t = jnp.concatenate(peers, axis=0).astype(BF16)
    load_pool.wait()
    for ab in range(9):
        part = dot(fine_t, pool_ref[:, ab * 128 : (ab + 1) * 128])
        wide = jnp.concatenate([part[24 * p : 24 * p + 24] for p in range(8)], axis=1)
        target = odd_ref if ab % 2 else even_ref
        target[24 * (ab // 2) : 24 * (ab // 2) + 24] = wide
    flat_ref[...] = jnp.zeros(flat_ref.shape, F32)
    lhs = [even_ref[...].astype(BF16), odd_ref[...].astype(BF16)]
    found = {}
    for k in range(3):
        for parity in range(2):
            value = dot(lhs[parity], rhs_ref[2 * k + (9 * k + parity) % 2])
            for i in range(5 - parity):
                found[9 * k + 2 * i + parity] = value[24 * i : 24 * i + 24]

    def place(tile, value):
        for r in range(3):
            flat_ref[pl.ds(42 * r + tile, 8, stride=128), :] = value[8 * r : 8 * r + 8]

    for n in range(0, TAPS, 2):
        tile = 3 * (n // 2)
        place(tile, found[n][:, :128])
        if n + 1 < TAPS:
            place(tile + 1, found[n][:, 128:] + found[n + 1][:, :128])
            place(tile + 2, found[n + 1][:, 128:])
        else:
            place(tile + 1, found[n][:, 128:])
    short = short.astype(BF16)
    for x in range(4):
        out_ref[x, :256] = flat_ref[256 * x : 256 * x + 256].astype(BF16)
        out_ref[x, 256:] = short


def sum_x_kernel(got_ref, out_ref):
    total = got_ref[0].astype(F32)
    for i in range(1, 4):
        total = total + got_ref[i].astype(F32)
    total = total.astype(BF16)
    for zh in range(2):
        for zl in range(8):
            row = 128 * zh + 16 * zl
            out_ref[2 * zl + zh, :16] = total[row : row + 16]
            rest = total[256 + 16 * zl : 272 + 16 * zl] if zl < 5 else jnp.zeros((16, 128), BF16)
            out_ref[2 * zl + zh, 16:] = rest


def sum_z_kernel(got_ref, out_ref):
    total = got_ref[0].astype(F32)
    for i in range(1, 16):
        total = total + got_ref[i].astype(F32)
    total = total.astype(BF16)
    for i in range(32):
        out_ref[i] = total


def assemble_kernel(got_ref, conv_ref, short_ref, gain_ref, flat_ref):
    for j in range(8):
        for zl in range(8):
            row = 128 * j + 16 * zl
            flat_ref[row : row + 16] = got_ref[8 * j + zl, :16].astype(F32)
        rest = jnp.concatenate([got_ref[8 * j + zl, 16:] for zl in range(5)], axis=0).astype(F32)
        for i in range(3):
            short_ref[24 * j : 24 * j + 24, 128 * i : 128 * i + 128] = rest[24 * i : 24 * i + 24]
        if j == 0:
            gain_ref[...] = jnp.concatenate([rest[72:73], rest[73:74, :64]], axis=1)
    for tile in range(TILES):
        wide = 128 if tile < TILES - 1 else 64
        for r in range(3):
            value = flat_ref[pl.ds(42 * r + tile, 8, stride=128), :]
            conv_ref[8 * r : 8 * r + 8, 128 * tile : 128 * tile + wide] = value[:, :wide]


def forward_kernel(
    before_ref, s_ref, act_ref, ds_ref, pos_hbm, w_short_hbm, gain_hbm, spread_hbm, w_conv_hbm,
    decoded_ref, grad_latent_ref,
    pos_ref, w_short_ref, gain_ref, spread_ref, w_conv_ref, z_all, sems,
):
    loads = [
        pltpu.make_async_copy(source, target, sems.at[i])
        for i, (source, target) in enumerate([
            (pos_hbm, pos_ref), (w_short_hbm, w_short_ref), (gain_hbm, gain_ref), (spread_hbm, spread_ref),
            (w_conv_hbm, w_conv_ref),
        ])
    ]
    for load in loads:
        load.start()
    for load in loads[:3]:
        load.wait()
    w_short = w_short_ref[...]
    grad_latent_ref[...] = dot(ds_ref[...], w_short).astype(BF16)
    prev = features(before_ref[...], w_short, gain_ref[...])[-1].astype(F32)
    act = act_ref[...]
    valid = [[(pos_ref[0, t] >= 2 - k).astype(F32) for k in range(2)] for t in range(2)]
    taps = [
        jnp.concatenate([prev[:CELLS] * valid[0][0], prev[CELLS:] * valid[1][0]], axis=0).astype(BF16),
        jnp.concatenate([prev[CELLS:] * valid[0][1], act[:CELLS].astype(F32) * valid[1][1]], axis=0).astype(BF16),
        act,
    ]
    loads[4].wait()
    for ab in range(9):
        acc = dot(taps[0], w_conv_ref[ab]) + dot(taps[1], w_conv_ref[9 + ab]) + dot(taps[2], w_conv_ref[18 + ab])
        if ab == 4:
            acc = acc + s_ref[...]
        z_all[64 * ab : 64 * ab + 64] = acc.astype(BF16)
    loads[3].wait()
    decoded_ref[...] = dot(spread_ref[...], z_all[...]).astype(BF16)


def shape(*dims, dtype=BF16):
    return jax.ShapeDtypeStruct(dims, dtype)


def in_hbm(value):
    return pltpu.with_memory_space_constraint(value, pltpu.HBM)


def call(kernel, name, outs, in_specs, scratch=()):
    return pl.pallas_call(
        kernel,
        out_shape=outs,
        in_specs=in_specs,
        out_specs=jax.tree.map(lambda _: VMEM, outs),
        scratch_shapes=list(scratch),
        compiler_params=pltpu.CompilerParams(vmem_limit_bytes=40 * 1024 * 1024),
        name=name,
    )


SMEM = pl.BlockSpec(memory_space=pltpu.SMEM)
VMEM = pl.BlockSpec(memory_space=pltpu.VMEM)
HBM = pl.BlockSpec(memory_space=pltpu.HBM)


def on_device(latent, frame_pos, w_short, gain, w_conv, cotangent):
    lat = latent.reshape(2 * CELLS, C_IN)
    cot = cotangent.reshape(2 * FINE, C)
    gain2 = gain.reshape(1, C)
    w27 = w_conv.reshape(TAPS, C, C)
    w_short_t = jnp.transpose(w_short)
    pool = jnp.asarray(pool_matrix(4), BF16)
    spread = jnp.asarray(pool_matrix(2), BF16)

    tm = ("zl", "y", "c")
    back = [(i + 1, i) for i in range(63)]
    following = lax.ppermute(cot, tm, back)
    next_pos = lax.ppermute(frame_pos, tm, back)
    before = lax.ppermute(lat, tm, [(i, i + 1) for i in range(63)])

    send, s_val, act, ds_flat = call(
        local_kernel, "local_kernel",
        [shape(8, SEND_ROWS, 128), shape(2 * CELLS, C, dtype=F32), shape(2 * CELLS, C), shape(2 * CELLS, C)],
        [SMEM, VMEM] + [HBM] * 7,
        [
            pltpu.SMEM((1, 2), jnp.int32), pltpu.VMEM((2 * CELLS, C_IN), BF16), pltpu.VMEM((C, C_IN), BF16),
            pltpu.VMEM((1, C), F32), pltpu.VMEM((2 * FINE, C), BF16), pltpu.VMEM((4 * FINE, 9 * 128), BF16),
            pltpu.VMEM((TAPS, C, C), BF16), pltpu.VMEM((4, C, 128), F32), pltpu.VMEM((9, C, 128), BF16),
            pltpu.SemaphoreType.DMA((7,)),
        ],
    )(next_pos, following, *map(in_hbm, (frame_pos, lat, w_short_t, gain2, cot, pool, w27)))
    got = lax.all_to_all(send, ("c", "y"), 0, 0)
    part = call(
        kernel_grad_kernel, "kernel_grad_kernel", shape(4, MSG, 128), [VMEM, HBM],
        [
            pltpu.VMEM((4 * FINE, 9 * 128), BF16), pltpu.VMEM((120, 1024), F32), pltpu.VMEM((96, 1024), F32),
            pltpu.VMEM((6, 1024, 256), BF16), pltpu.VMEM((1024, 128), F32), pltpu.SemaphoreType.DMA,
        ],
    )(got, in_hbm(pool))
    got = lax.all_to_all(part, "x", 0, 0)
    part = call(sum_x_kernel, "sum_x_kernel", shape(16, 32, 128), [VMEM])(got)
    got = lax.all_to_all(part, ("zl", "zh"), 0, 0)
    part = call(sum_z_kernel, "sum_z_kernel", shape(32, 32, 128), [VMEM])(got)
    got = lax.all_to_all(part, ("y", "zl"), 0, 0)
    got = lax.all_gather(got, "c", axis=0, tiled=True)
    grad_conv, grad_short_t, grad_gain = call(
        assemble_kernel, "assemble_kernel",
        [shape(24, TAPS * C, dtype=F32), shape(C, C_IN, dtype=F32), shape(1, C, dtype=F32)],
        [VMEM], [pltpu.VMEM((1024, 128), F32)],
    )(got)

    decoded, grad_latent = call(
        forward_kernel, "forward_kernel", [shape(2 * FINE, C), shape(2 * CELLS, C_IN)],
        [VMEM] * 4 + [HBM] * 5,
        [
            pltpu.SMEM((1, 2), jnp.int32), pltpu.VMEM((C, C_IN), BF16), pltpu.VMEM((1, C), F32),
            pltpu.VMEM((2 * FINE, 18 * CELLS), BF16), pltpu.VMEM((TAPS, C, C), BF16),
            pltpu.VMEM((9 * 2 * CELLS, C), BF16), pltpu.SemaphoreType.DMA((5,)),
        ],
    )(before, s_val, act, ds_flat, *map(in_hbm, (frame_pos, w_short_t, gain2, spread, w27)))
    return (
        decoded.reshape(cotangent.shape),
        grad_latent.reshape(latent.shape),
        grad_conv,
        jnp.transpose(grad_short_t),
        grad_gain.reshape(C),
    )


def solution(mesh):
    fine = Mesh(mesh.devices.reshape(8, 4, 2, 4, 2), ("zl", "y", "c", "x", "zh"))
    tm, dp = ("zl", "y", "c"), ("x", "zh")
    return jax.shard_map(
        on_device,
        mesh=fine,
        in_specs=(
            P(dp, tm, None, None, None),
            P(dp, tm),
            P(),
            P(),
            P(),
            P(dp, tm, None, None, None),
        ),
        out_specs=(
            P(dp, tm, None, None, None),
            P(dp, tm, None, None, None),
            P(dp, None),
            P(),
            P(),
        ),
        check_vma=False,
    )
```

```python
import jax
import jax.numpy as jnp
import numpy as np
from jax import lax
from jax.experimental import pallas as pl
from jax.experimental.pallas import tpu as pltpu
from jax.sharding import Mesh, PartitionSpec as P

EPS = 1e-06
C_IN = 384
C = 192
CELLS = 32
FINE = 128
TAPS = 27
TILES = 41
SHORT_ROWS = 80
SEND_ROWS = 192 + SHORT_ROWS
MSG = 256 + SHORT_ROWS
BF16 = jnp.bfloat16
F32 = jnp.float32


def pool_matrix(frames):
    out = np.zeros((frames, 8, 16, 3, 3, frames, 4, 8), np.float32)
    for t in range(frames):
        for a in range(3):
            for b in range(3):
                for p in range(8):
                    for q in range(16):
                        row, col = p + a - 1, q + b - 1
                        if 0 <= row < 8 and 0 <= col < 16:
                            out[t, p, q, a, b, t, row // 2, col // 2] = 1
    return out.reshape(frames * FINE, 9 * frames * CELLS)


def dot(a, b):
    return jnp.dot(a, b, preferred_element_type=F32)


def dot_nt(a, b):
    return lax.dot_general(a, b, (((1,), (1,)), ((), ())), preferred_element_type=F32)


def activation(s_val, gain):
    scale = lax.rsqrt(jnp.mean(s_val * s_val, axis=-1, keepdims=True) + EPS)
    normed = s_val * scale
    z_val = normed * gain
    return scale, normed, z_val, 1.0 / (1.0 + jnp.exp(-z_val))


def features(inputs, w_short_t, gain):
    s_val = dot_nt(inputs, w_short_t)
    _, _, z_val, sig = activation(s_val, gain)
    return s_val, (z_val * sig).astype(BF16)


def start_loads(pairs, sems):
    loads = [pltpu.make_async_copy(source, target, sems.at[i]) for i, (source, target) in enumerate(pairs)]
    for load in loads:
        load.start()
    return loads


def slices_for(turned_ref, tiles, j):
    return jnp.concatenate(
        [turned_ref[t, pl.ds(8 * r + j, 8, stride=24), :] for t in tiles for r in range(3)], axis=0
    ).astype(BF16)


def ahead_kernel(pos_hbm, cot_hbm, ahead_ref, pos_ref, cot_ref, sems):
    for load in start_loads([(pos_hbm, pos_ref), (cot_hbm, cot_ref)], sems):
        load.wait()
    keep = [(pos_ref[:, t : t + 1] >= t + 1).astype(F32) for t in range(2)]
    for t in range(2):
        rows = slice(FINE * t, FINE * t + FINE)
        ahead_ref[rows] = (cot_ref[rows].astype(F32) * keep[t]).astype(BF16)


def own_kernel(
    lat_hbm, w_short_hbm, gain_hbm, cot_hbm, pos_hbm, pool_hbm, w_conv_hbm,
    send_ref, s_ref, act_ref, ct_ref, pooled_ref, pool_ref, w_conv_ref, lat_ref, gain_ref, pos_ref,
    w_short_ref, cot_ref, turned_ref, sems,
):
    loads = start_loads([
        (lat_hbm, lat_ref), (w_short_hbm, w_short_ref), (gain_hbm, gain_ref), (cot_hbm, cot_ref),
        (pool_hbm, pool_ref), (w_conv_hbm, w_conv_ref), (pos_hbm, pos_ref),
    ], sems)
    loads[3].wait()
    fine_t = jnp.transpose(cot_ref[...].astype(F32))
    for t in range(2):
        turned_ref[t] = fine_t[:, 128 * t : 128 * t + 128]
    for load in loads[:3]:
        load.wait()
    s_val, act = features(lat_ref[...], w_short_ref[...], gain_ref[...])
    s_ref[...] = s_val
    act_ref[...] = act
    tail = jnp.concatenate([act[:CELLS, 128:], act[CELLS:, 128:]], axis=1)
    packed = jnp.concatenate([act[:, :128], tail], axis=0)

    for j in range(8):
        send_ref[j, :48] = slices_for(turned_ref, (0, 1), j)
        send_ref[j, 96:192] = packed

    fine_t = fine_t.astype(BF16)
    loads[4].wait()
    for ab in range(9):
        part = dot(fine_t, pool_ref[: 2 * FINE, ab * 128 : (ab + 1) * 128])
        if ab == 4:
            pooled_ref[...] = jnp.transpose(part)[: 2 * CELLS]
        ct_ref[ab] = part.astype(BF16)
    loads[5].wait()
    loads[6].wait()


def local_kernel(
    next_ref, sent_ref, s_ref, ct_ref, pooled_ref, pool_ref, w_conv_ref, lat_ref, gain_ref, pos_ref,
    send_ref, ds_ref, turned_ref,
):
    fine_t = jnp.transpose(next_ref[...].astype(F32))
    for t in range(2):
        turned_ref[t] = fine_t[:, 128 * t : 128 * t + 128]
    for j in range(8):
        send_ref[j, :48] = sent_ref[j, :48]
        send_ref[j, 48:96] = slices_for(turned_ref, (0, 1), j)
        send_ref[j, 96:192] = sent_ref[j, 96:192]

    fine_t = fine_t.astype(BF16)
    acc = None
    for ab in range(9):
        part = dot(fine_t, pool_ref[2 * FINE :, ab * 128 : (ab + 1) * 128]).astype(BF16)
        pooled = ct_ref[ab] + part
        taps = jnp.concatenate([w_conv_ref[9 * k + ab] for k in range(3)], axis=0)
        value = dot(taps, pooled)
        acc = value if acc is None else acc + value
    turned = [jnp.transpose(acc[C * k : C * k + C]) for k in range(3)]
    follows = (pos_ref[:, 1:] >= 1).astype(F32)
    gain = gain_ref[...]
    early = turned[2][:32] + follows * (turned[1][32:64] + turned[0][64:96])
    late = turned[2][32:64] + turned[1][64:96] + turned[0][96:]
    grad_act = jnp.concatenate([early, late], axis=0)
    scale, normed, z_val, sig = activation(s_ref[...], gain)
    dz_val = grad_act * sig * (1.0 + z_val * (1.0 - sig))
    gain_term = jnp.sum(dz_val * normed, axis=0, keepdims=True)
    dn_val = dz_val * gain
    ds_val = scale * (dn_val - normed * jnp.mean(dn_val * normed, axis=-1, keepdims=True)) + pooled_ref[...]
    ds_ref[...] = ds_val.astype(BF16)

    short_t = dot(jnp.transpose(ds_val).astype(BF16), lat_ref[...])
    last = jnp.concatenate(
        [gain_term[:, :128], jnp.concatenate([gain_term[:, 128:], jnp.zeros((1, 64), F32)], axis=1),
         jnp.broadcast_to(follows, (1, 128)), jnp.zeros((5, 128), F32)], axis=0)
    for j in range(8):
        rows = short_t[24 * j : 24 * j + 24]
        flat = jnp.concatenate([rows[:, :128], rows[:, 128:256], rows[:, 256:], last], axis=0)
        send_ref[j, 192:] = flat.astype(BF16)


def kernel_grad_kernel(got_ref, pool_ref, out_ref, even_ref, odd_ref, rhs_ref, flat_ref):
    none = jnp.zeros((CELLS, C), F32)
    gap = jnp.zeros((4 * CELLS, 64), F32)
    peers = []
    short = jnp.zeros((SHORT_ROWS, 128), F32)
    for p in range(8):
        block = got_ref[p, :96].astype(F32)
        peers.append(jnp.concatenate([block[24 * i : 24 * i + 24] for i in range(4)], axis=1))
        tail = got_ref[p, 160:192].astype(F32)
        act = jnp.concatenate(
            [got_ref[p, 96:160].astype(F32), jnp.concatenate([tail[:, :64], tail[:, 64:]], axis=0)], axis=1)
        extra = got_ref[p, 192:].astype(F32)
        short = short + extra
        act0, act1 = act[:CELLS], act[CELLS:]
        mine = act0 * extra[74:75, :1]
        rows = [[none, none, mine, act1], [none, mine, act1, none], [act0, act1, none, none]]
        for k in range(3):
            value = jnp.concatenate(rows[k], axis=0)
            rhs_ref[2 * k, 128 * p : 128 * p + 128] = jnp.concatenate([value, gap], axis=1).astype(BF16)
            rhs_ref[2 * k + 1, 128 * p : 128 * p + 128] = jnp.concatenate([gap, value], axis=1).astype(BF16)
    fine_t = jnp.concatenate(peers, axis=0).astype(BF16)
    for ab in range(9):
        part = dot(fine_t, pool_ref[:, ab * 128 : (ab + 1) * 128])
        wide = jnp.concatenate([part[24 * p : 24 * p + 24] for p in range(8)], axis=1)
        target = odd_ref if ab % 2 else even_ref
        target[24 * (ab // 2) : 24 * (ab // 2) + 24] = wide
    flat_ref[...] = jnp.zeros(flat_ref.shape, F32)
    lhs = [even_ref[...].astype(BF16), odd_ref[...].astype(BF16)]
    found = {}
    for k in range(3):
        for parity in range(2):
            value = dot(lhs[parity], rhs_ref[2 * k + (9 * k + parity) % 2])
            for i in range(5 - parity):
                found[9 * k + 2 * i + parity] = value[24 * i : 24 * i + 24]

    def place(tile, value):
        for r in range(3):
            flat_ref[pl.ds(42 * r + tile, 8, stride=128), :] = value[8 * r : 8 * r + 8]

    for n in range(0, TAPS, 2):
        tile = 3 * (n // 2)
        place(tile, found[n][:, :128])
        if n + 1 < TAPS:
            place(tile + 1, found[n][:, 128:] + found[n + 1][:, :128])
            place(tile + 2, found[n + 1][:, 128:])
        else:
            place(tile + 1, found[n][:, 128:])
    short = short.astype(BF16)
    for x in range(4):
        out_ref[x, :256] = flat_ref[256 * x : 256 * x + 256].astype(BF16)
        out_ref[x, 256:] = short


def sum_x_kernel(got_ref, lat_ref, out_ref, lat_out_ref):
    lat_out_ref[...] = lat_ref[...]
    total = got_ref[0].astype(F32)
    for i in range(1, 4):
        total = total + got_ref[i].astype(F32)
    total = total.astype(BF16)
    for zh in range(2):
        for zl in range(8):
            row = 128 * zh + 16 * zl
            out_ref[2 * zl + zh, :16] = total[row : row + 16]
            rest = total[256 + 16 * zl : 272 + 16 * zl] if zl < 5 else jnp.zeros((16, 128), BF16)
            out_ref[2 * zl + zh, 16:] = rest


def sum_z_kernel(got_ref, turn_ref, out_ref):
    total = got_ref[0].astype(F32)
    for i in range(1, 16):
        total = total + got_ref[i].astype(F32)
    total = total.astype(BF16)
    for i in range(32):
        out_ref[i] = total


def assemble_kernel(got_ref, conv_ref, short_ref, gain_ref, flat_ref):
    for j in range(8):
        for zl in range(8):
            row = 128 * j + 16 * zl
            flat_ref[row : row + 16] = got_ref[8 * j + zl, :16].astype(F32)
        rest = jnp.concatenate([got_ref[8 * j + zl, 16:] for zl in range(5)], axis=0).astype(F32)
        for i in range(3):
            short_ref[24 * j : 24 * j + 24, 128 * i : 128 * i + 128] = rest[24 * i : 24 * i + 24]
        if j == 0:
            gain_ref[...] = jnp.concatenate([rest[72:73], rest[73:74, :64]], axis=1)
    for tile in range(TILES):
        wide = 128 if tile < TILES - 1 else 64
        for r in range(3):
            value = flat_ref[pl.ds(42 * r + tile, 8, stride=128), :]
            conv_ref[8 * r : 8 * r + 8, 128 * tile : 128 * tile + wide] = value[:, :wide]


def forward_kernel(
    before_ref, s_ref, act_ref, ds_ref, w_conv_ref, pos_hbm, w_short_hbm, gain_hbm, spread_hbm,
    decoded_ref, grad_latent_ref,
    pos_ref, w_short_ref, gain_ref, spread_ref, z_all, sems,
):
    loads = start_loads([
        (pos_hbm, pos_ref), (w_short_hbm, w_short_ref), (gain_hbm, gain_ref), (spread_hbm, spread_ref),
    ], sems)
    for load in loads[:3]:
        load.wait()
    w_short = w_short_ref[...]
    grad_latent_ref[...] = dot(ds_ref[...], w_short).astype(BF16)
    prev = features(before_ref[...], w_short, gain_ref[...])[-1].astype(F32)
    act = act_ref[...]
    valid = [[(pos_ref[0, t] >= 2 - k).astype(F32) for k in range(2)] for t in range(2)]
    taps = [
        jnp.concatenate([prev[:CELLS] * valid[0][0], prev[CELLS:] * valid[1][0]], axis=0).astype(BF16),
        jnp.concatenate([prev[CELLS:] * valid[0][1], act[:CELLS].astype(F32) * valid[1][1]], axis=0).astype(BF16),
        act,
    ]
    for ab in range(9):
        acc = dot(taps[0], w_conv_ref[ab]) + dot(taps[1], w_conv_ref[9 + ab]) + dot(taps[2], w_conv_ref[18 + ab])
        if ab == 4:
            acc = acc + s_ref[...]
        z_all[64 * ab : 64 * ab + 64] = acc.astype(BF16)
    loads[3].wait()
    decoded_ref[...] = dot(spread_ref[...], z_all[...]).astype(BF16)


def shape(*dims, dtype=BF16):
    return jax.ShapeDtypeStruct(dims, dtype)


def in_hbm(value):
    return pltpu.with_memory_space_constraint(value, pltpu.HBM)


def call(kernel, name, outs, in_specs, scratch=()):
    return pl.pallas_call(
        kernel,
        out_shape=outs,
        in_specs=in_specs,
        out_specs=jax.tree.map(lambda _: VMEM, outs),
        scratch_shapes=list(scratch),
        compiler_params=pltpu.CompilerParams(vmem_limit_bytes=40 * 1024 * 1024),
        name=name,
    )


VMEM = pl.BlockSpec(memory_space=pltpu.VMEM)
HBM = pl.BlockSpec(memory_space=pltpu.HBM)
ANY = pl.BlockSpec(memory_space=pl.ANY)


def on_device(latent, frame_pos, w_short, gain, w_conv, cotangent):
    lat = latent.reshape(2 * CELLS, C_IN)
    cot = cotangent.reshape(2 * FINE, C)
    gain2 = gain.reshape(1, C)
    w27 = w_conv.reshape(TAPS, C, C)
    w_short_t = jnp.transpose(w_short)
    pool = jnp.asarray(pool_matrix(4), BF16)
    spread = jnp.asarray(pool_matrix(2), BF16)

    tm = ("zl", "y", "c")
    ahead = call(
        ahead_kernel, "ahead_kernel", shape(2 * FINE, C), [HBM, HBM],
        [pltpu.VMEM((1, 2), jnp.int32), pltpu.VMEM((2 * FINE, C), BF16), pltpu.SemaphoreType.DMA((2,))],
    )(in_hbm(frame_pos), in_hbm(cot))
    following = lax.ppermute(ahead, tm, [(i + 1, i) for i in range(63)])
    own, s_val, act, ct, pooled, pool_near, conv_near, lat_near, gain_near, pos_near = call(
        own_kernel, "own_kernel",
        [
            shape(8, SEND_ROWS, 128), shape(2 * CELLS, C, dtype=F32), shape(2 * CELLS, C), shape(9, C, 128),
            shape(2 * CELLS, C, dtype=F32), shape(4 * FINE, 9 * 128), shape(TAPS, C, C),
            shape(2 * CELLS, C_IN), shape(1, C, dtype=F32), shape(1, 2, dtype=jnp.int32),
        ],
        [HBM] * 7,
        [
            pltpu.VMEM((C, C_IN), BF16), pltpu.VMEM((2 * FINE, C), BF16), pltpu.VMEM((2, C, 128), F32),
            pltpu.SemaphoreType.DMA((7,)),
        ],
    )(*map(in_hbm, (lat, w_short_t, gain2, cot, frame_pos, pool, w27)))
    send, ds_flat = call(
        local_kernel, "local_kernel", [shape(8, SEND_ROWS, 128), shape(2 * CELLS, C)],
        [VMEM] * 10, [pltpu.VMEM((2, C, 128), F32)],
    )(following, own, s_val, ct, pooled, pool_near, conv_near, lat_near, gain_near, pos_near)
    got = lax.all_to_all(send, ("c", "y"), 0, 0)
    part = call(
        kernel_grad_kernel, "kernel_grad_kernel", shape(4, MSG, 128), [VMEM, VMEM],
        [
            pltpu.VMEM((120, 1024), F32), pltpu.VMEM((96, 1024), F32),
            pltpu.VMEM((6, 1024, 256), BF16), pltpu.VMEM((1024, 128), F32),
        ],
    )(got, pool_near)
    got = lax.all_to_all(part, "x", 0, 0)
    part, lat_late = call(
        sum_x_kernel, "sum_x_kernel", [shape(16, 32, 128), shape(2 * CELLS, C_IN)], [VMEM, VMEM]
    )(got, lat_near)
    before = lax.ppermute(lat_late, tm, [(i, i + 1) for i in range(63)])
    decoded, grad_latent = call(
        forward_kernel, "forward_kernel", [shape(2 * FINE, C), shape(2 * CELLS, C_IN)],
        [VMEM] * 5 + [HBM] * 4,
        [
            pltpu.SMEM((1, 2), jnp.int32), pltpu.VMEM((C, C_IN), BF16), pltpu.VMEM((1, C), F32),
            pltpu.VMEM((2 * FINE, 18 * CELLS), BF16), pltpu.VMEM((9 * 2 * CELLS, C), BF16),
            pltpu.SemaphoreType.DMA((4,)),
        ],
    )(before, s_val, act, ds_flat, conv_near, *map(in_hbm, (frame_pos, w_short_t, gain2, spread)))
    got = lax.all_to_all(part, ("zl", "zh"), 0, 0)
    part = call(sum_z_kernel, "sum_z_kernel", shape(32, 32, 128), [VMEM, ANY])(got, in_hbm(grad_latent))
    got = lax.all_to_all(part, ("y", "zl"), 0, 0)
    got = lax.all_gather(got, "c", axis=0, tiled=True)
    grad_conv, grad_short_t, grad_gain = call(
        assemble_kernel, "assemble_kernel",
        [shape(24, TAPS * C, dtype=F32), shape(C, C_IN, dtype=F32), shape(1, C, dtype=F32)],
        [VMEM], [pltpu.VMEM((1024, 128), F32)],
    )(got)
    return (
        decoded.reshape(cotangent.shape),
        grad_latent.reshape(latent.shape),
        grad_conv,
        jnp.transpose(grad_short_t),
        grad_gain.reshape(C),
    )


def solution(mesh):
    fine = Mesh(mesh.devices.reshape(8, 4, 2, 4, 2), ("zl", "y", "c", "x", "zh"))
    tm, dp = ("zl", "y", "c"), ("x", "zh")
    return jax.shard_map(
        on_device,
        mesh=fine,
        in_specs=(
            P(dp, tm, None, None, None),
            P(dp, tm),
            P(),
            P(),
            P(),
            P(dp, tm, None, None, None),
        ),
        out_specs=(
            P(dp, tm, None, None, None),
            P(dp, tm, None, None, None),
            P(dp, None),
            P(),
            P(),
        ),
        check_vma=False,
    )
```

```python
import jax
import jax.numpy as jnp
import numpy as np
from jax import lax
from jax.experimental import pallas as pl
from jax.experimental.pallas import tpu as pltpu
from jax.sharding import Mesh, PartitionSpec as P

EPS = 1e-06
C_IN = 384
C = 192
CELLS = 32
FINE = 128
TAPS = 27
TILES = 41
SHORT_ROWS = 80
SEND_ROWS = 192 + SHORT_ROWS
MSG = 256 + SHORT_ROWS
BF16 = jnp.bfloat16
F32 = jnp.float32


def pool_matrix(frames):
    out = np.zeros((frames, 8, 16, 3, 3, frames, 4, 8), np.float32)
    for t in range(frames):
        for a in range(3):
            for b in range(3):
                for p in range(8):
                    for q in range(16):
                        row, col = p + a - 1, q + b - 1
                        if 0 <= row < 8 and 0 <= col < 16:
                            out[t, p, q, a, b, t, row // 2, col // 2] = 1
    return out.reshape(frames * FINE, 9 * frames * CELLS)


def dot(a, b):
    return jnp.dot(a, b, preferred_element_type=F32)


def dot_nt(a, b):
    return lax.dot_general(a, b, (((1,), (1,)), ((), ())), preferred_element_type=F32)


def activation(s_val, gain):
    scale = lax.rsqrt(jnp.mean(s_val * s_val, axis=-1, keepdims=True) + EPS)
    normed = s_val * scale
    z_val = normed * gain
    return scale, normed, z_val, 1.0 / (1.0 + jnp.exp(-z_val))


def features(inputs, w_short_t, gain):
    s_val = dot_nt(inputs, w_short_t)
    _, _, z_val, sig = activation(s_val, gain)
    return s_val, (z_val * sig).astype(BF16)


def start_loads(pairs, sems):
    loads = [pltpu.make_async_copy(source, target, sems.at[i]) for i, (source, target) in enumerate(pairs)]
    for load in loads:
        load.start()
    return loads


def slices_for(turned_ref, tiles, j):
    return jnp.concatenate(
        [turned_ref[t, pl.ds(8 * r + j, 8, stride=24), :] for t in tiles for r in range(3)], axis=0
    ).astype(BF16)


def ahead_kernel(pos_hbm, cot_hbm, ahead_ref, pos_ref, cot_ref, sems):
    for load in start_loads([(pos_hbm, pos_ref), (cot_hbm, cot_ref)], sems):
        load.wait()
    keep = [(pos_ref[:, t : t + 1] >= t + 1).astype(F32) for t in range(2)]
    for t in range(2):
        rows = slice(FINE * t, FINE * t + FINE)
        ahead_ref[rows] = (cot_ref[rows].astype(F32) * keep[t]).astype(BF16)


def two_taps(w_conv_ref, k, ab):
    return jnp.concatenate([w_conv_ref[9 * k + ab], w_conv_ref[9 * k + 9 + ab]], axis=0)


def own_kernel(
    lat_hbm, w_short_hbm, gain_hbm, cot_hbm, pos_hbm, pool_hbm, w_conv_hbm,
    send_ref, s_ref, act_ref, turned_own_ref, pooled_ref, pool_ref, w_conv_ref, lat_ref, gain_ref, pos_ref,
    w_short_ref, cot_ref, turned_ref, sems,
):
    loads = start_loads([
        (lat_hbm, lat_ref), (w_short_hbm, w_short_ref), (gain_hbm, gain_ref), (cot_hbm, cot_ref),
        (pool_hbm, pool_ref), (w_conv_hbm, w_conv_ref), (pos_hbm, pos_ref),
    ], sems)
    loads[3].wait()
    fine_t = jnp.transpose(cot_ref[...].astype(F32))
    for t in range(2):
        turned_ref[t] = fine_t[:, 128 * t : 128 * t + 128]
    for load in loads[:3]:
        load.wait()
    s_val, act = features(lat_ref[...], w_short_ref[...], gain_ref[...])
    s_ref[...] = s_val
    act_ref[...] = act
    tail = jnp.concatenate([act[:CELLS, 128:], act[CELLS:, 128:]], axis=1)
    packed = jnp.concatenate([act[:, :128], tail], axis=0)

    for j in range(8):
        send_ref[j, :48] = slices_for(turned_ref, (0, 1), j)
        send_ref[j, 96:192] = packed

    fine_t = fine_t.astype(BF16)
    loads[4].wait()
    loads[5].wait()
    acc = None
    for ab in range(9):
        part = dot(fine_t, pool_ref[: 2 * FINE, ab * 128 : (ab + 1) * 128])
        if ab == 4:
            pooled_ref[...] = jnp.transpose(part)[: 2 * CELLS]
        value = dot(two_taps(w_conv_ref, 1, ab), part.astype(BF16))
        acc = value if acc is None else acc + value
    for i in range(2):
        turned_own_ref[i] = jnp.transpose(acc[C * i : C * i + C])
    loads[6].wait()


def local_kernel(
    next_ref, sent_ref, s_ref, turned_own_ref, pooled_ref, pool_ref, w_conv_ref, lat_ref, gain_ref, pos_ref,
    send_ref, ds_ref, turned_ref,
):
    fine_t = jnp.transpose(next_ref[...].astype(F32))
    for t in range(2):
        turned_ref[t] = fine_t[:, 128 * t : 128 * t + 128]
    for j in range(8):
        send_ref[j, :48] = sent_ref[j, :48]
        send_ref[j, 48:96] = slices_for(turned_ref, (0, 1), j)
        send_ref[j, 96:192] = sent_ref[j, 96:192]

    fine_t = fine_t.astype(BF16)
    acc = None
    for ab in range(9):
        part = dot(fine_t, pool_ref[2 * FINE :, ab * 128 : (ab + 1) * 128])
        value = dot(two_taps(w_conv_ref, 0, ab), part.astype(BF16))
        acc = value if acc is None else acc + value
    after = [jnp.transpose(acc[C * i : C * i + C]) for i in range(2)]
    tap1, tap2 = turned_own_ref[0], turned_own_ref[1]
    follows = (pos_ref[:, 1:] >= 1).astype(F32)
    gain = gain_ref[...]
    early = tap2[:32] + follows * (tap1[32:64] + after[0][64:96])
    late = tap2[32:64] + after[1][64:96] + after[0][96:]
    grad_act = jnp.concatenate([early, late], axis=0)
    scale, normed, z_val, sig = activation(s_ref[...], gain)
    dz_val = grad_act * sig * (1.0 + z_val * (1.0 - sig))
    gain_term = jnp.sum(dz_val * normed, axis=0, keepdims=True)
    dn_val = dz_val * gain
    ds_val = scale * (dn_val - normed * jnp.mean(dn_val * normed, axis=-1, keepdims=True)) + pooled_ref[...]
    ds_ref[...] = ds_val.astype(BF16)

    short_t = dot(jnp.transpose(ds_val).astype(BF16), lat_ref[...])
    flag = jnp.broadcast_to(follows, (1, 128))
    for j in range(8):
        piece = gain_term[:, 64 * (j % 3) : 64 * (j % 3) + 64]
        spare = 176 + 8 * (j // 4)
        flat = jnp.concatenate([
            short_t[24 * j : 24 * j + 24, :128], short_t[24 * j : 24 * j + 24, 128:256],
            short_t[22 * j : 22 * j + 22, 256:], short_t[spare : spare + 8, 256:],
            jnp.concatenate([piece, piece], axis=1), flag,
        ], axis=0)
        send_ref[j, 192:] = flat.astype(BF16)


def kernel_grad_kernel(got_ref, pool_ref, out_ref, even_ref, odd_ref, rhs_ref, flat_ref):
    none = jnp.zeros((CELLS, C), F32)
    gap = jnp.zeros((4 * CELLS, 64), F32)
    peers = []
    short = jnp.zeros((SHORT_ROWS, 128), F32)
    for p in range(8):
        block = got_ref[p, :96].astype(F32)
        peers.append(jnp.concatenate([block[24 * i : 24 * i + 24] for i in range(4)], axis=1))
        tail = got_ref[p, 160:192].astype(F32)
        act = jnp.concatenate(
            [got_ref[p, 96:160].astype(F32), jnp.concatenate([tail[:, :64], tail[:, 64:]], axis=0)], axis=1)
        extra = got_ref[p, 192:].astype(F32)
        short = short + extra
        act0, act1 = act[:CELLS], act[CELLS:]
        mine = act0 * extra[79:80, :1]
        rows = [[none, none, mine, act1], [none, mine, act1, none], [act0, act1, none, none]]
        for k in range(3):
            value = jnp.concatenate(rows[k], axis=0)
            rhs_ref[2 * k, 128 * p : 128 * p + 128] = jnp.concatenate([value, gap], axis=1).astype(BF16)
            rhs_ref[2 * k + 1, 128 * p : 128 * p + 128] = jnp.concatenate([gap, value], axis=1).astype(BF16)
    fine_t = jnp.concatenate(peers, axis=0).astype(BF16)
    for ab in range(9):
        part = dot(fine_t, pool_ref[:, ab * 128 : (ab + 1) * 128])
        wide = jnp.concatenate([part[24 * p : 24 * p + 24] for p in range(8)], axis=1)
        target = odd_ref if ab % 2 else even_ref
        target[24 * (ab // 2) : 24 * (ab // 2) + 24] = wide
    flat_ref[...] = jnp.zeros(flat_ref.shape, F32)
    lhs = [even_ref[...].astype(BF16), odd_ref[...].astype(BF16)]
    found = {}
    for k in range(3):
        for parity in range(2):
            value = dot(lhs[parity], rhs_ref[2 * k + (9 * k + parity) % 2])
            for i in range(5 - parity):
                found[9 * k + 2 * i + parity] = value[24 * i : 24 * i + 24]

    def place(tile, value):
        for r in range(3):
            flat_ref[pl.ds(40 * r + tile, 8, stride=128), :] = value[8 * r : 8 * r + 8]

    for n in range(0, TAPS, 2):
        tile = 3 * (n // 2)
        place(tile, found[n][:, :128])
        if n + 1 < TAPS:
            place(tile + 1, found[n][:, 128:] + found[n + 1][:, :128])
            place(tile + 2, found[n + 1][:, 128:])
        else:
            half = found[n][:, 128:192]
            gain_piece = jnp.broadcast_to(short[78:79, 64:], (8, 64))
            flat_ref[pl.ds(120, 8, stride=128), :] = jnp.concatenate([half[:8], half[8:16]], axis=1)
            flat_ref[pl.ds(121, 8, stride=128), :] = jnp.concatenate([half[16:], gain_piece], axis=1)
    short = short.astype(BF16)
    for x in range(4):
        out_ref[x, :256] = flat_ref[256 * x : 256 * x + 256].astype(BF16)
        out_ref[x, 256:] = short


def sum_x_kernel(got_ref, out_ref):
    total = got_ref[0].astype(F32)
    for i in range(1, 4):
        total = total + got_ref[i].astype(F32)
    for zh in range(2):
        chunks = jnp.concatenate([total[128 * zh : 128 * zh + 122], total[256:326]], axis=0)
        for zl in range(8):
            piece = jnp.concatenate([chunks[24 * zl : 24 * zl + 24], total[326:334]], axis=0)
            out_ref[8 * zh + zl] = piece.astype(BF16)


def sum_z_kernel(got_ref, lat_ref, out_ref, spare_ref, lat_out_ref):
    lat_out_ref[...] = lat_ref[...]
    total = got_ref[0].astype(F32)
    for i in range(1, 16):
        total = total + got_ref[i].astype(F32)
    piece = total[:24].astype(BF16)
    for i in range(32):
        out_ref[i] = piece
    spare_ref[...] = total[24:].astype(BF16)


def assemble_kernel(got_ref, spare_ref, conv_ref, short_ref, gain_ref, flat_ref):
    for j in range(8):
        for zl in range(8):
            row = 192 * j + 24 * zl
            flat_ref[row : row + 24] = got_ref[32 * (j // 4) + 4 * zl + j % 4].astype(F32)
    for tile in range(TILES - 1):
        for r in range(3):
            value = flat_ref[pl.ds(40 * r + tile, 8, stride=192), :]
            conv_ref[8 * r : 8 * r + 8, 128 * tile : 128 * tile + 128] = value
    halves = [flat_ref[pl.ds(120 + i, 8, stride=192), :] for i in range(2)]
    conv_ref[:, 128 * TILES - 128 :] = jnp.concatenate([halves[0][:, :64], halves[0][:, 64:], halves[1][:, :64]], axis=0)
    gain_ref[...] = jnp.concatenate([halves[1][m : m + 1, 64:] for m in range(3)], axis=1)
    for j in range(8):
        row = 192 * j + 122
        short_ref[24 * j : 24 * j + 24, :128] = flat_ref[row : row + 24]
        short_ref[24 * j : 24 * j + 24, 128:256] = flat_ref[row + 24 : row + 48]
        short_ref[22 * j : 22 * j + 22, 256:] = flat_ref[row + 48 : row + 70]
    short_ref[176:, 256:] = spare_ref[...].astype(F32)


def forward_kernel(
    before_ref, s_ref, act_ref, ds_ref, w_conv_ref, pos_hbm, w_short_hbm, gain_hbm, spread_hbm,
    decoded_ref, grad_latent_ref,
    pos_ref, w_short_ref, gain_ref, spread_ref, z_all, sems,
):
    loads = start_loads([
        (pos_hbm, pos_ref), (w_short_hbm, w_short_ref), (gain_hbm, gain_ref), (spread_hbm, spread_ref),
    ], sems)
    for load in loads[:3]:
        load.wait()
    w_short = w_short_ref[...]
    grad_latent_ref[...] = dot(ds_ref[...], w_short).astype(BF16)
    prev = features(before_ref[...], w_short, gain_ref[...])[-1].astype(F32)
    act = act_ref[...]
    valid = [[(pos_ref[0, t] >= 2 - k).astype(F32) for k in range(2)] for t in range(2)]
    taps = [
        jnp.concatenate([prev[:CELLS] * valid[0][0], prev[CELLS:] * valid[1][0]], axis=0).astype(BF16),
        jnp.concatenate([prev[CELLS:] * valid[0][1], act[:CELLS].astype(F32) * valid[1][1]], axis=0).astype(BF16),
        act,
    ]
    for ab in range(9):
        acc = dot(taps[0], w_conv_ref[ab]) + dot(taps[1], w_conv_ref[9 + ab]) + dot(taps[2], w_conv_ref[18 + ab])
        if ab == 4:
            acc = acc + s_ref[...]
        z_all[64 * ab : 64 * ab + 64] = acc.astype(BF16)
    loads[3].wait()
    decoded_ref[...] = dot(spread_ref[...], z_all[...]).astype(BF16)


def shape(*dims, dtype=BF16):
    return jax.ShapeDtypeStruct(dims, dtype)


def in_hbm(value):
    return pltpu.with_memory_space_constraint(value, pltpu.HBM)


def call(kernel, name, outs, in_specs, scratch=()):
    return pl.pallas_call(
        kernel,
        out_shape=outs,
        in_specs=in_specs,
        out_specs=jax.tree.map(lambda _: VMEM, outs),
        scratch_shapes=list(scratch),
        compiler_params=pltpu.CompilerParams(vmem_limit_bytes=40 * 1024 * 1024),
        name=name,
    )


VMEM = pl.BlockSpec(memory_space=pltpu.VMEM)
HBM = pl.BlockSpec(memory_space=pltpu.HBM)
ANY = pl.BlockSpec(memory_space=pl.ANY)


def on_device(latent, frame_pos, w_short, gain, w_conv, cotangent):
    lat = latent.reshape(2 * CELLS, C_IN)
    cot = cotangent.reshape(2 * FINE, C)
    gain2 = gain.reshape(1, C)
    w27 = w_conv.reshape(TAPS, C, C)
    w_short_t = jnp.transpose(w_short)
    pool = jnp.asarray(pool_matrix(4), BF16)
    spread = jnp.asarray(pool_matrix(2), BF16)

    tm = ("zl", "y", "c")
    ahead = call(
        ahead_kernel, "ahead_kernel", shape(2 * FINE, C), [HBM, HBM],
        [pltpu.VMEM((1, 2), jnp.int32), pltpu.VMEM((2 * FINE, C), BF16), pltpu.SemaphoreType.DMA((2,))],
    )(in_hbm(frame_pos), in_hbm(cot))
    following = lax.ppermute(ahead, tm, [(i + 1, i) for i in range(63)])
    own, s_val, act, turned_own, pooled, pool_near, conv_near, lat_near, gain_near, pos_near = call(
        own_kernel, "own_kernel",
        [
            shape(8, SEND_ROWS, 128), shape(2 * CELLS, C, dtype=F32), shape(2 * CELLS, C), shape(2, 128, C, dtype=F32),
            shape(2 * CELLS, C, dtype=F32), shape(4 * FINE, 9 * 128), shape(TAPS, C, C),
            shape(2 * CELLS, C_IN), shape(1, C, dtype=F32), shape(1, 2, dtype=jnp.int32),
        ],
        [HBM] * 7,
        [
            pltpu.VMEM((C, C_IN), BF16), pltpu.VMEM((2 * FINE, C), BF16), pltpu.VMEM((2, C, 128), F32),
            pltpu.SemaphoreType.DMA((7,)),
        ],
    )(*map(in_hbm, (lat, w_short_t, gain2, cot, frame_pos, pool, w27)))
    send, ds_flat = call(
        local_kernel, "local_kernel", [shape(8, SEND_ROWS, 128), shape(2 * CELLS, C)],
        [VMEM] * 10, [pltpu.VMEM((2, C, 128), F32)],
    )(following, own, s_val, turned_own, pooled, pool_near, conv_near, lat_near, gain_near, pos_near)
    got = lax.all_to_all(send, ("c", "y"), 0, 0)
    part = call(
        kernel_grad_kernel, "kernel_grad_kernel", shape(4, MSG, 128), [VMEM, VMEM],
        [
            pltpu.VMEM((120, 1024), F32), pltpu.VMEM((96, 1024), F32),
            pltpu.VMEM((6, 1024, 256), BF16), pltpu.VMEM((1024, 128), F32),
        ],
    )(got, pool_near)
    got = lax.all_to_all(part, "x", 0, 0)
    part = call(sum_x_kernel, "sum_x_kernel", shape(16, 32, 128), [VMEM])(got)
    got = lax.all_to_all(part, ("zh", "zl"), 0, 0)
    part, spare, lat_late = call(
        sum_z_kernel, "sum_z_kernel", [shape(32, 24, 128), shape(8, 128), shape(2 * CELLS, C_IN)], [VMEM, VMEM]
    )(got, lat_near)
    before = lax.ppermute(lat_late, tm, [(i, i + 1) for i in range(63)])
    decoded, grad_latent = call(
        forward_kernel, "forward_kernel", [shape(2 * FINE, C), shape(2 * CELLS, C_IN)],
        [VMEM] * 5 + [HBM] * 4,
        [
            pltpu.SMEM((1, 2), jnp.int32), pltpu.VMEM((C, C_IN), BF16), pltpu.VMEM((1, C), F32),
            pltpu.VMEM((2 * FINE, 18 * CELLS), BF16), pltpu.VMEM((9 * 2 * CELLS, C), BF16),
            pltpu.SemaphoreType.DMA((4,)),
        ],
    )(before, s_val, act, ds_flat, conv_near, *map(in_hbm, (frame_pos, w_short_t, gain2, spread)))
    got = lax.all_to_all(part, ("zl", "y"), 0, 0)
    got = lax.all_gather(got, "c", axis=0, tiled=True)
    spare = lax.all_gather(spare, "c", axis=0, tiled=True)
    grad_conv, grad_short_t, grad_gain = call(
        assemble_kernel, "assemble_kernel",
        [shape(24, TAPS * C, dtype=F32), shape(C, C_IN, dtype=F32), shape(1, C, dtype=F32)],
        [VMEM, VMEM], [pltpu.VMEM((1536, 128), F32)],
    )(got, spare)
    return (
        decoded.reshape(cotangent.shape),
        grad_latent.reshape(latent.shape),
        grad_conv,
        jnp.transpose(grad_short_t),
        grad_gain.reshape(C),
    )


def solution(mesh):
    fine = Mesh(mesh.devices.reshape(8, 4, 2, 4, 2), ("zl", "y", "c", "x", "zh"))
    tm, dp = ("zl", "y", "c"), ("x", "zh")
    return jax.shard_map(
        on_device,
        mesh=fine,
        in_specs=(
            P(dp, tm, None, None, None),
            P(dp, tm),
            P(),
            P(),
            P(),
            P(dp, tm, None, None, None),
        ),
        out_specs=(
            P(dp, tm, None, None, None),
            P(dp, tm, None, None, None),
            P(dp, None),
            P(),
            P(),
        ),
        check_vma=False,
    )
```

```python
import jax
import jax.numpy as jnp
import numpy as np
from jax import lax
from jax.experimental import pallas as pl
from jax.experimental.pallas import tpu as pltpu
from jax.sharding import Mesh, PartitionSpec as P

EPS = 1e-06
C_IN = 384
C = 192
CELLS = 32
FINE = 128
TAPS = 27
Z_FIRST = 10
ZL_ORDER = (4, 3, 5, 2, 6, 1, 7, 0)
TILES = 41
SHORT_ROWS = 80
SEND_ROWS = 192 + SHORT_ROWS
MSG = 256 + SHORT_ROWS
BF16 = jnp.bfloat16
F32 = jnp.float32


def pool_matrix(frames):
    out = np.zeros((frames, 8, 16, 3, 3, frames, 4, 8), np.float32)
    for t in range(frames):
        for a in range(3):
            for b in range(3):
                for p in range(8):
                    for q in range(16):
                        row, col = p + a - 1, q + b - 1
                        if 0 <= row < 8 and 0 <= col < 16:
                            out[t, p, q, a, b, t, row // 2, col // 2] = 1
    return out.reshape(frames * FINE, 9 * frames * CELLS)


def dot(a, b):
    return jnp.dot(a, b, preferred_element_type=F32)


def dot_nt(a, b):
    return lax.dot_general(a, b, (((1,), (1,)), ((), ())), preferred_element_type=F32)


def activation(s_val, gain):
    scale = lax.rsqrt(jnp.mean(s_val * s_val, axis=-1, keepdims=True) + EPS)
    normed = s_val * scale
    z_val = normed * gain
    return scale, normed, z_val, 1.0 / (1.0 + jnp.exp(-z_val))


def features(inputs, w_short_t, gain):
    s_val = dot_nt(inputs, w_short_t)
    _, _, z_val, sig = activation(s_val, gain)
    return s_val, (z_val * sig).astype(BF16)


def start_loads(pairs, sems):
    loads = [pltpu.make_async_copy(source, target, sems.at[i]) for i, (source, target) in enumerate(pairs)]
    for load in loads:
        load.start()
    return loads


def slices_for(turned_ref, tiles, j):
    return jnp.concatenate(
        [turned_ref[t, pl.ds(8 * r + j, 8, stride=24), :] for t in tiles for r in range(3)], axis=0
    ).astype(BF16)


def ahead_kernel(pos_hbm, cot_hbm, ahead_ref, pos_ref, cot_ref, sems):
    for load in start_loads([(pos_hbm, pos_ref), (cot_hbm, cot_ref)], sems):
        load.wait()
    keep = [(pos_ref[:, t : t + 1] >= t + 1).astype(F32) for t in range(2)]
    for t in range(2):
        rows = slice(FINE * t, FINE * t + FINE)
        ahead_ref[rows] = (cot_ref[rows].astype(F32) * keep[t]).astype(BF16)


def two_taps(w_conv_ref, k, ab):
    return jnp.concatenate([w_conv_ref[9 * k + ab], w_conv_ref[9 * k + 9 + ab]], axis=0)


def own_kernel(
    lat_hbm, w_short_hbm, gain_hbm, cot_hbm, pos_hbm, pool_hbm, w_conv_hbm,
    send_ref, s_ref, act_ref, turned_own_ref, pooled_ref, pool_ref, w_conv_ref, lat_ref, gain_ref, pos_ref,
    w_short_ref, cot_ref, turned_ref, sems,
):
    loads = start_loads([
        (lat_hbm, lat_ref), (w_short_hbm, w_short_ref), (gain_hbm, gain_ref), (cot_hbm, cot_ref),
        (pool_hbm, pool_ref), (w_conv_hbm, w_conv_ref), (pos_hbm, pos_ref),
    ], sems)
    loads[3].wait()
    fine_t = jnp.transpose(cot_ref[...].astype(F32))
    for t in range(2):
        turned_ref[t] = fine_t[:, 128 * t : 128 * t + 128]
    for load in loads[:3]:
        load.wait()
    s_val, act = features(lat_ref[...], w_short_ref[...], gain_ref[...])
    s_ref[...] = s_val
    act_ref[...] = act
    tail = jnp.concatenate([act[:CELLS, 128:], act[CELLS:, 128:]], axis=1)
    packed = jnp.concatenate([act[:, :128], tail], axis=0)

    for j in range(8):
        send_ref[j, :48] = slices_for(turned_ref, (0, 1), j)
        send_ref[j, 96:192] = packed

    fine_t = fine_t.astype(BF16)
    loads[4].wait()
    loads[5].wait()
    acc = None
    for ab in range(9):
        part = dot(fine_t, pool_ref[: 2 * FINE, ab * 128 : (ab + 1) * 128])
        if ab == 4:
            pooled_ref[...] = jnp.transpose(part)[: 2 * CELLS]
        value = dot(two_taps(w_conv_ref, 1, ab), part.astype(BF16))
        acc = value if acc is None else acc + value
    for i in range(2):
        turned_own_ref[i] = jnp.transpose(acc[C * i : C * i + C])
    loads[6].wait()


def local_kernel(
    next_ref, sent_ref, s_ref, turned_own_ref, pooled_ref, pool_ref, w_conv_ref, lat_ref, gain_ref, pos_ref,
    send_ref, ds_ref, turned_ref,
):
    fine_t = jnp.transpose(next_ref[...].astype(F32))
    for t in range(2):
        turned_ref[t] = fine_t[:, 128 * t : 128 * t + 128]
    for j in range(8):
        send_ref[j, :48] = sent_ref[j, :48]
        send_ref[j, 48:96] = slices_for(turned_ref, (0, 1), j)
        send_ref[j, 96:192] = sent_ref[j, 96:192]

    fine_t = fine_t.astype(BF16)
    acc = None
    for ab in range(9):
        part = dot(fine_t, pool_ref[2 * FINE :, ab * 128 : (ab + 1) * 128])
        value = dot(two_taps(w_conv_ref, 0, ab), part.astype(BF16))
        acc = value if acc is None else acc + value
    after = [jnp.transpose(acc[C * i : C * i + C]) for i in range(2)]
    tap1, tap2 = turned_own_ref[0], turned_own_ref[1]
    follows = (pos_ref[:, 1:] >= 1).astype(F32)
    gain = gain_ref[...]
    early = tap2[:32] + follows * (tap1[32:64] + after[0][64:96])
    late = tap2[32:64] + after[1][64:96] + after[0][96:]
    grad_act = jnp.concatenate([early, late], axis=0)
    scale, normed, z_val, sig = activation(s_ref[...], gain)
    dz_val = grad_act * sig * (1.0 + z_val * (1.0 - sig))
    gain_term = jnp.sum(dz_val * normed, axis=0, keepdims=True)
    dn_val = dz_val * gain
    ds_val = scale * (dn_val - normed * jnp.mean(dn_val * normed, axis=-1, keepdims=True)) + pooled_ref[...]
    ds_ref[...] = ds_val.astype(BF16)

    short_t = dot(jnp.transpose(ds_val).astype(BF16), lat_ref[...])
    flag = jnp.broadcast_to(follows, (1, 128))
    for j in range(8):
        piece = gain_term[:, 64 * (j % 3) : 64 * (j % 3) + 64]
        spare = 176 + 8 * (j // 4)
        flat = jnp.concatenate([
            short_t[24 * j : 24 * j + 24, :128], short_t[24 * j : 24 * j + 24, 128:256],
            short_t[22 * j : 22 * j + 22, 256:], short_t[spare : spare + 8, 256:],
            jnp.concatenate([piece, piece], axis=1), flag,
        ], axis=0)
        send_ref[j, 192:] = flat.astype(BF16)


def kernel_grad_kernel(got_ref, pool_ref, out_ref, even_ref, odd_ref, rhs_ref, flat_ref):
    none = jnp.zeros((CELLS, C), F32)
    gap = jnp.zeros((4 * CELLS, 64), F32)
    peers = []
    short = jnp.zeros((SHORT_ROWS, 128), F32)
    for p in range(8):
        block = got_ref[p, :96].astype(F32)
        peers.append(jnp.concatenate([block[24 * i : 24 * i + 24] for i in range(4)], axis=1))
        tail = got_ref[p, 160:192].astype(F32)
        act = jnp.concatenate(
            [got_ref[p, 96:160].astype(F32), jnp.concatenate([tail[:, :64], tail[:, 64:]], axis=0)], axis=1)
        extra = got_ref[p, 192:].astype(F32)
        short = short + extra
        act0, act1 = act[:CELLS], act[CELLS:]
        mine = act0 * extra[79:80, :1]
        rows = [[none, none, mine, act1], [none, mine, act1, none], [act0, act1, none, none]]
        for k in range(3):
            value = jnp.concatenate(rows[k], axis=0)
            rhs_ref[2 * k, 128 * p : 128 * p + 128] = jnp.concatenate([value, gap], axis=1).astype(BF16)
            rhs_ref[2 * k + 1, 128 * p : 128 * p + 128] = jnp.concatenate([gap, value], axis=1).astype(BF16)
    fine_t = jnp.concatenate(peers, axis=0).astype(BF16)
    for ab in range(9):
        part = dot(fine_t, pool_ref[:, ab * 128 : (ab + 1) * 128])
        wide = jnp.concatenate([part[24 * p : 24 * p + 24] for p in range(8)], axis=1)
        target = odd_ref if ab % 2 else even_ref
        target[24 * (ab // 2) : 24 * (ab // 2) + 24] = wide
    flat_ref[...] = jnp.zeros(flat_ref.shape, F32)
    lhs = [even_ref[...].astype(BF16), odd_ref[...].astype(BF16)]
    found = {}
    for k in range(3):
        for parity in range(2):
            value = dot(lhs[parity], rhs_ref[2 * k + (9 * k + parity) % 2])
            for i in range(5 - parity):
                found[9 * k + 2 * i + parity] = value[24 * i : 24 * i + 24]

    def place(tile, value):
        for r in range(3):
            flat_ref[pl.ds(40 * r + tile, 8, stride=128), :] = value[8 * r : 8 * r + 8]

    for n in range(0, TAPS, 2):
        tile = 3 * (n // 2)
        place(tile, found[n][:, :128])
        if n + 1 < TAPS:
            place(tile + 1, found[n][:, 128:] + found[n + 1][:, :128])
            place(tile + 2, found[n + 1][:, 128:])
        else:
            half = found[n][:, 128:192]
            gain_piece = jnp.broadcast_to(short[78:79, 64:], (8, 64))
            flat_ref[pl.ds(120, 8, stride=128), :] = jnp.concatenate([half[:8], half[8:16]], axis=1)
            flat_ref[pl.ds(121, 8, stride=128), :] = jnp.concatenate([half[16:], gain_piece], axis=1)
    short = short.astype(BF16)
    for x in range(4):
        out_ref[x, :256] = flat_ref[256 * x : 256 * x + 256].astype(BF16)
        out_ref[x, 256:] = short


def sum_x_kernel(got_ref, out_ref):
    total = got_ref[0].astype(F32)
    for i in range(1, 4):
        total = total + got_ref[i].astype(F32)
    for zh in range(2):
        chunks = jnp.concatenate([total[128 * zh : 128 * zh + 122], total[256:326]], axis=0)
        for zl in range(8):
            piece = jnp.concatenate([chunks[24 * zl : 24 * zl + 24], total[326:334]], axis=0)
            out_ref[(8 * zh + zl - Z_FIRST) % 16] = piece.astype(BF16)


def sum_z_kernel(got_ref, lat_ref, out_ref, spare_ref, lat_out_ref):
    lat_out_ref[...] = lat_ref[...]
    total = got_ref[0].astype(F32)
    for i in range(1, 16):
        total = total + got_ref[i].astype(F32)
    piece = total[:24].astype(BF16)
    for i in range(32):
        out_ref[i] = piece
    spare_ref[...] = total[24:].astype(BF16)


def assemble_kernel(got_ref, spare_ref, conv_ref, short_ref, gain_ref, flat_ref):
    for j in range(8):
        for zl in range(8):
            row = 192 * j + 24 * zl
            flat_ref[row : row + 24] = got_ref[32 * (j // 4) + 4 * ZL_ORDER.index(zl) + j % 4].astype(F32)
    for tile in range(TILES - 1):
        for r in range(3):
            value = flat_ref[pl.ds(40 * r + tile, 8, stride=192), :]
            conv_ref[8 * r : 8 * r + 8, 128 * tile : 128 * tile + 128] = value
    halves = [flat_ref[pl.ds(120 + i, 8, stride=192), :] for i in range(2)]
    conv_ref[:, 128 * TILES - 128 :] = jnp.concatenate([halves[0][:, :64], halves[0][:, 64:], halves[1][:, :64]], axis=0)
    gain_ref[...] = jnp.concatenate([halves[1][m : m + 1, 64:] for m in range(3)], axis=1)
    for j in range(8):
        row = 192 * j + 122
        short_ref[24 * j : 24 * j + 24, :128] = flat_ref[row : row + 24]
        short_ref[24 * j : 24 * j + 24, 128:256] = flat_ref[row + 24 : row + 48]
        short_ref[22 * j : 22 * j + 22, 256:] = flat_ref[row + 48 : row + 70]
    short_ref[176:, 256:] = spare_ref[...].astype(F32)


def forward_kernel(
    before_ref, s_ref, act_ref, ds_ref, w_conv_ref, pos_hbm, w_short_hbm, gain_hbm, spread_hbm,
    decoded_ref, grad_latent_ref,
    pos_ref, w_short_ref, gain_ref, spread_ref, z_all, sems,
):
    loads = start_loads([
        (pos_hbm, pos_ref), (w_short_hbm, w_short_ref), (gain_hbm, gain_ref), (spread_hbm, spread_ref),
    ], sems)
    for load in loads[:3]:
        load.wait()
    w_short = w_short_ref[...]
    grad_latent_ref[...] = dot(ds_ref[...], w_short).astype(BF16)
    prev = features(before_ref[...], w_short, gain_ref[...])[-1].astype(F32)
    act = act_ref[...]
    valid = [[(pos_ref[0, t] >= 2 - k).astype(F32) for k in range(2)] for t in range(2)]
    taps = [
        jnp.concatenate([prev[:CELLS] * valid[0][0], prev[CELLS:] * valid[1][0]], axis=0).astype(BF16),
        jnp.concatenate([prev[CELLS:] * valid[0][1], act[:CELLS].astype(F32) * valid[1][1]], axis=0).astype(BF16),
        act,
    ]
    for ab in range(9):
        acc = dot(taps[0], w_conv_ref[ab]) + dot(taps[1], w_conv_ref[9 + ab]) + dot(taps[2], w_conv_ref[18 + ab])
        if ab == 4:
            acc = acc + s_ref[...]
        z_all[64 * ab : 64 * ab + 64] = acc.astype(BF16)
    loads[3].wait()
    decoded_ref[...] = dot(spread_ref[...], z_all[...]).astype(BF16)


def shape(*dims, dtype=BF16):
    return jax.ShapeDtypeStruct(dims, dtype)


def in_hbm(value):
    return pltpu.with_memory_space_constraint(value, pltpu.HBM)


def call(kernel, name, outs, in_specs, scratch=()):
    return pl.pallas_call(
        kernel,
        out_shape=outs,
        in_specs=in_specs,
        out_specs=jax.tree.map(lambda _: VMEM, outs),
        scratch_shapes=list(scratch),
        compiler_params=pltpu.CompilerParams(vmem_limit_bytes=40 * 1024 * 1024),
        name=name,
    )


VMEM = pl.BlockSpec(memory_space=pltpu.VMEM)
HBM = pl.BlockSpec(memory_space=pltpu.HBM)
ANY = pl.BlockSpec(memory_space=pl.ANY)


def on_device(latent, frame_pos, w_short, gain, w_conv, cotangent):
    lat = latent.reshape(2 * CELLS, C_IN)
    cot = cotangent.reshape(2 * FINE, C)
    gain2 = gain.reshape(1, C)
    w27 = w_conv.reshape(TAPS, C, C)
    w_short_t = jnp.transpose(w_short)
    pool = jnp.asarray(pool_matrix(4), BF16)
    spread = jnp.asarray(pool_matrix(2), BF16)

    tm = ("zl", "y", "c")
    ahead = call(
        ahead_kernel, "ahead_kernel", shape(2 * FINE, C), [HBM, HBM],
        [pltpu.VMEM((1, 2), jnp.int32), pltpu.VMEM((2 * FINE, C), BF16), pltpu.SemaphoreType.DMA((2,))],
    )(in_hbm(frame_pos), in_hbm(cot))
    following = lax.ppermute(ahead, tm, [(i + 1, i) for i in range(63)])
    own, s_val, act, turned_own, pooled, pool_near, conv_near, lat_near, gain_near, pos_near = call(
        own_kernel, "own_kernel",
        [
            shape(8, SEND_ROWS, 128), shape(2 * CELLS, C, dtype=F32), shape(2 * CELLS, C), shape(2, 128, C, dtype=F32),
            shape(2 * CELLS, C, dtype=F32), shape(4 * FINE, 9 * 128), shape(TAPS, C, C),
            shape(2 * CELLS, C_IN), shape(1, C, dtype=F32), shape(1, 2, dtype=jnp.int32),
        ],
        [HBM] * 7,
        [
            pltpu.VMEM((C, C_IN), BF16), pltpu.VMEM((2 * FINE, C), BF16), pltpu.VMEM((2, C, 128), F32),
            pltpu.SemaphoreType.DMA((7,)),
        ],
    )(*map(in_hbm, (lat, w_short_t, gain2, cot, frame_pos, pool, w27)))
    send, ds_flat = call(
        local_kernel, "local_kernel", [shape(8, SEND_ROWS, 128), shape(2 * CELLS, C)],
        [VMEM] * 10, [pltpu.VMEM((2, C, 128), F32)],
    )(following, own, s_val, turned_own, pooled, pool_near, conv_near, lat_near, gain_near, pos_near)
    got = lax.all_to_all(send, ("c", "y"), 0, 0)
    part = call(
        kernel_grad_kernel, "kernel_grad_kernel", shape(4, MSG, 128), [VMEM, VMEM],
        [
            pltpu.VMEM((120, 1024), F32), pltpu.VMEM((96, 1024), F32),
            pltpu.VMEM((6, 1024, 256), BF16), pltpu.VMEM((1024, 128), F32),
        ],
    )(got, pool_near)
    got = lax.all_to_all(part, "x", 0, 0)
    part = call(sum_x_kernel, "sum_x_kernel", shape(16, 32, 128), [VMEM])(got)
    got = lax.all_to_all(part, ("zh", "zl"), 0, 0, axis_index_groups=[[(Z_FIRST + i) % 16 for i in range(16)]])
    part, spare, lat_late = call(
        sum_z_kernel, "sum_z_kernel", [shape(32, 24, 128), shape(8, 128), shape(2 * CELLS, C_IN)], [VMEM, VMEM]
    )(got, lat_near)
    before = lax.ppermute(lat_late, tm, [(i, i + 1) for i in range(63)])
    decoded, grad_latent = call(
        forward_kernel, "forward_kernel", [shape(2 * FINE, C), shape(2 * CELLS, C_IN)],
        [VMEM] * 5 + [HBM] * 4,
        [
            pltpu.SMEM((1, 2), jnp.int32), pltpu.VMEM((C, C_IN), BF16), pltpu.VMEM((1, C), F32),
            pltpu.VMEM((2 * FINE, 18 * CELLS), BF16), pltpu.VMEM((9 * 2 * CELLS, C), BF16),
            pltpu.SemaphoreType.DMA((4,)),
        ],
    )(before, s_val, act, ds_flat, conv_near, *map(in_hbm, (frame_pos, w_short_t, gain2, spread)))
    got = lax.all_to_all(part, ("zl", "y"), 0, 0, axis_index_groups=[[4 * zl + y for zl in ZL_ORDER for y in range(4)]])
    got = lax.all_gather(got, "c", axis=0, tiled=True)
    spare = lax.all_gather(spare, "c", axis=0, tiled=True)
    grad_conv, grad_short_t, grad_gain = call(
        assemble_kernel, "assemble_kernel",
        [shape(24, TAPS * C, dtype=F32), shape(C, C_IN, dtype=F32), shape(1, C, dtype=F32)],
        [VMEM, VMEM], [pltpu.VMEM((1536, 128), F32)],
    )(got, spare)
    return (
        decoded.reshape(cotangent.shape),
        grad_latent.reshape(latent.shape),
        grad_conv,
        jnp.transpose(grad_short_t),
        grad_gain.reshape(C),
    )


def solution(mesh):
    fine = Mesh(mesh.devices.reshape(8, 4, 2, 4, 2), ("zl", "y", "c", "x", "zh"))
    tm, dp = ("zl", "y", "c"), ("x", "zh")
    return jax.shard_map(
        on_device,
        mesh=fine,
        in_specs=(
            P(dp, tm, None, None, None),
            P(dp, tm),
            P(),
            P(),
            P(),
            P(dp, tm, None, None, None),
        ),
        out_specs=(
            P(dp, tm, None, None, None),
            P(dp, tm, None, None, None),
            P(dp, None),
            P(),
            P(),
        ),
        check_vma=False,
    )
```

```python
import jax
import jax.numpy as jnp
import numpy as np
from jax import lax
from jax.experimental import pallas as pl
from jax.experimental.pallas import tpu as pltpu
from jax.sharding import Mesh, PartitionSpec as P

EPS = 1e-06
C_IN = 384
C = 192
CELLS = 32
FINE = 128
TAPS = 27
Z_FIRST = 10
ZL_ORDER = (4, 3, 5, 2, 6, 1, 7, 0)
TILES = 41
SHORT_ROWS = 80
SEND_ROWS = 192 + SHORT_ROWS
MSG = 256 + SHORT_ROWS
BF16 = jnp.bfloat16
F32 = jnp.float32


def pool_matrix(frames):
    out = np.zeros((frames, 8, 16, 3, 3, frames, 4, 8), np.float32)
    for t in range(frames):
        for a in range(3):
            for b in range(3):
                for p in range(8):
                    for q in range(16):
                        row, col = p + a - 1, q + b - 1
                        if 0 <= row < 8 and 0 <= col < 16:
                            out[t, p, q, a, b, t, row // 2, col // 2] = 1
    return out.reshape(frames * FINE, 9 * frames * CELLS)


def dot(a, b):
    return jnp.dot(a, b, preferred_element_type=F32)


def dot_nt(a, b):
    return lax.dot_general(a, b, (((1,), (1,)), ((), ())), preferred_element_type=F32)


def activation(s_val, gain):
    scale = lax.rsqrt(jnp.mean(s_val * s_val, axis=-1, keepdims=True) + EPS)
    normed = s_val * scale
    z_val = normed * gain
    return scale, normed, z_val, 1.0 / (1.0 + jnp.exp(-z_val))


def features(inputs, w_short_t, gain):
    s_val = dot_nt(inputs, w_short_t)
    _, _, z_val, sig = activation(s_val, gain)
    return s_val, (z_val * sig).astype(BF16)


def start_loads(pairs, sems):
    loads = [pltpu.make_async_copy(source, target, sems.at[i]) for i, (source, target) in enumerate(pairs)]
    for load in loads:
        load.start()
    return loads


def slices_for(turned_ref, tiles, j):
    return jnp.concatenate(
        [turned_ref[t, pl.ds(8 * r + j, 8, stride=24), :] for t in tiles for r in range(3)], axis=0
    ).astype(BF16)


def ahead_kernel(pos_hbm, cot_hbm, ahead_ref, pos_ref, cot_ref, sems):
    for load in start_loads([(pos_hbm, pos_ref), (cot_hbm, cot_ref)], sems):
        load.wait()
    keep = [(pos_ref[:, t : t + 1] >= t + 1).astype(F32) for t in range(2)]
    for t in range(2):
        rows = slice(FINE * t, FINE * t + FINE)
        ahead_ref[rows] = (cot_ref[rows].astype(F32) * keep[t]).astype(BF16)


def two_taps(w_conv_ref, k, ab):
    return jnp.concatenate([w_conv_ref[9 * k + ab], w_conv_ref[9 * k + 9 + ab]], axis=0)


def own_kernel(
    lat_hbm, w_short_hbm, gain_hbm, cot_hbm, pos_hbm, pool_hbm, w_conv_hbm, spread_hbm,
    send_ref, s_ref, act_ref, turned_own_ref, pooled_ref, pool_ref, w_conv_ref, lat_ref, gain_ref, pos_ref,
    w_short_ref, spread_ref, cot_ref, turned_ref, sems,
):
    loads = start_loads([
        (lat_hbm, lat_ref), (w_short_hbm, w_short_ref), (gain_hbm, gain_ref), (cot_hbm, cot_ref),
        (pool_hbm, pool_ref), (w_conv_hbm, w_conv_ref), (pos_hbm, pos_ref),
        (spread_hbm, spread_ref),
    ], sems)
    loads[3].wait()
    fine_t = jnp.transpose(cot_ref[...].astype(F32))
    for t in range(2):
        turned_ref[t] = fine_t[:, 128 * t : 128 * t + 128]
    for load in loads[:3]:
        load.wait()
    s_val, act = features(lat_ref[...], w_short_ref[...], gain_ref[...])
    s_ref[...] = s_val
    act_ref[...] = act
    tail = jnp.concatenate([act[:CELLS, 128:], act[CELLS:, 128:]], axis=1)
    packed = jnp.concatenate([act[:, :128], tail], axis=0)

    for j in range(8):
        send_ref[j, :48] = slices_for(turned_ref, (0, 1), j)
        send_ref[j, 96:192] = packed

    fine_t = fine_t.astype(BF16)
    loads[4].wait()
    loads[5].wait()
    acc = None
    for ab in range(9):
        part = dot(fine_t, pool_ref[: 2 * FINE, ab * 128 : (ab + 1) * 128])
        if ab == 4:
            pooled_ref[...] = jnp.transpose(part)[: 2 * CELLS]
        value = dot(two_taps(w_conv_ref, 1, ab), part.astype(BF16))
        acc = value if acc is None else acc + value
    for i in range(2):
        turned_own_ref[i] = jnp.transpose(acc[C * i : C * i + C])
    loads[6].wait()
    loads[7].wait()


def local_kernel(
    next_ref, sent_ref, s_ref, turned_own_ref, pooled_ref, pool_ref, w_conv_ref, lat_ref, gain_ref, pos_ref,
    send_ref, ds_ref, turned_ref,
):
    fine_t = jnp.transpose(next_ref[...].astype(F32))
    for t in range(2):
        turned_ref[t] = fine_t[:, 128 * t : 128 * t + 128]
    for j in range(8):
        send_ref[j, :48] = sent_ref[j, :48]
        send_ref[j, 48:96] = slices_for(turned_ref, (0, 1), j)
        send_ref[j, 96:192] = sent_ref[j, 96:192]

    fine_t = fine_t.astype(BF16)
    acc = None
    for ab in range(9):
        part = dot(fine_t, pool_ref[2 * FINE :, ab * 128 : (ab + 1) * 128])
        value = dot(two_taps(w_conv_ref, 0, ab), part.astype(BF16))
        acc = value if acc is None else acc + value
    after = [jnp.transpose(acc[C * i : C * i + C]) for i in range(2)]
    tap1, tap2 = turned_own_ref[0], turned_own_ref[1]
    follows = (pos_ref[:, 1:] >= 1).astype(F32)
    gain = gain_ref[...]
    early = tap2[:32] + follows * (tap1[32:64] + after[0][64:96])
    late = tap2[32:64] + after[1][64:96] + after[0][96:]
    grad_act = jnp.concatenate([early, late], axis=0)
    scale, normed, z_val, sig = activation(s_ref[...], gain)
    dz_val = grad_act * sig * (1.0 + z_val * (1.0 - sig))
    gain_term = jnp.sum(dz_val * normed, axis=0, keepdims=True)
    dn_val = dz_val * gain
    ds_val = scale * (dn_val - normed * jnp.mean(dn_val * normed, axis=-1, keepdims=True)) + pooled_ref[...]
    ds_ref[...] = ds_val.astype(BF16)

    short_t = dot(jnp.transpose(ds_val).astype(BF16), lat_ref[...])
    flag = jnp.broadcast_to(follows, (1, 128))
    for j in range(8):
        piece = gain_term[:, 64 * (j % 3) : 64 * (j % 3) + 64]
        spare = 176 + 8 * (j // 4)
        flat = jnp.concatenate([
            short_t[24 * j : 24 * j + 24, :128], short_t[24 * j : 24 * j + 24, 128:256],
            short_t[22 * j : 22 * j + 22, 256:], short_t[spare : spare + 8, 256:],
            jnp.concatenate([piece, piece], axis=1), flag,
        ], axis=0)
        send_ref[j, 192:] = flat.astype(BF16)


def kernel_grad_kernel(got_ref, pool_ref, out_ref, even_ref, odd_ref, rhs_ref, flat_ref):
    none = jnp.zeros((CELLS, C), F32)
    gap = jnp.zeros((4 * CELLS, 64), F32)
    peers = []
    short = jnp.zeros((SHORT_ROWS, 128), F32)
    for p in range(8):
        block = got_ref[p, :96].astype(F32)
        peers.append(jnp.concatenate([block[24 * i : 24 * i + 24] for i in range(4)], axis=1))
        tail = got_ref[p, 160:192].astype(F32)
        act = jnp.concatenate(
            [got_ref[p, 96:160].astype(F32), jnp.concatenate([tail[:, :64], tail[:, 64:]], axis=0)], axis=1)
        extra = got_ref[p, 192:].astype(F32)
        short = short + extra
        act0, act1 = act[:CELLS], act[CELLS:]
        mine = act0 * extra[79:80, :1]
        rows = [[none, none, mine, act1], [none, mine, act1, none], [act0, act1, none, none]]
        for k in range(3):
            value = jnp.concatenate(rows[k], axis=0)
            rhs_ref[2 * k, 128 * p : 128 * p + 128] = jnp.concatenate([value, gap], axis=1).astype(BF16)
            rhs_ref[2 * k + 1, 128 * p : 128 * p + 128] = jnp.concatenate([gap, value], axis=1).astype(BF16)
    fine_t = jnp.concatenate(peers, axis=0).astype(BF16)
    for ab in range(9):
        part = dot(fine_t, pool_ref[:, ab * 128 : (ab + 1) * 128])
        wide = jnp.concatenate([part[24 * p : 24 * p + 24] for p in range(8)], axis=1)
        target = odd_ref if ab % 2 else even_ref
        target[24 * (ab // 2) : 24 * (ab // 2) + 24] = wide
    flat_ref[...] = jnp.zeros(flat_ref.shape, F32)
    lhs = [even_ref[...].astype(BF16), odd_ref[...].astype(BF16)]
    found = {}
    for k in range(3):
        for parity in range(2):
            value = dot(lhs[parity], rhs_ref[2 * k + (9 * k + parity) % 2])
            for i in range(5 - parity):
                found[9 * k + 2 * i + parity] = value[24 * i : 24 * i + 24]

    def place(tile, value):
        for r in range(3):
            flat_ref[pl.ds(40 * r + tile, 8, stride=128), :] = value[8 * r : 8 * r + 8]

    for n in range(0, TAPS, 2):
        tile = 3 * (n // 2)
        place(tile, found[n][:, :128])
        if n + 1 < TAPS:
            place(tile + 1, found[n][:, 128:] + found[n + 1][:, :128])
            place(tile + 2, found[n + 1][:, 128:])
        else:
            half = found[n][:, 128:192]
            gain_piece = jnp.broadcast_to(short[78:79, 64:], (8, 64))
            flat_ref[pl.ds(120, 8, stride=128), :] = jnp.concatenate([half[:8], half[8:16]], axis=1)
            flat_ref[pl.ds(121, 8, stride=128), :] = jnp.concatenate([half[16:], gain_piece], axis=1)
    short = short.astype(BF16)
    for x in range(4):
        out_ref[x, :256] = flat_ref[256 * x : 256 * x + 256].astype(BF16)
        out_ref[x, 256:] = short


def sum_x_kernel(got_ref, out_ref):
    total = got_ref[0].astype(F32)
    for i in range(1, 4):
        total = total + got_ref[i].astype(F32)
    for zh in range(2):
        chunks = jnp.concatenate([total[128 * zh : 128 * zh + 122], total[256:326]], axis=0)
        for zl in range(8):
            piece = jnp.concatenate([chunks[24 * zl : 24 * zl + 24], total[326:334]], axis=0)
            out_ref[(8 * zh + zl - Z_FIRST) % 16] = piece.astype(BF16)


def sum_z_kernel(got_ref, lat_ref, out_ref, spare_ref, lat_out_ref):
    lat_out_ref[...] = lat_ref[...]
    total = got_ref[0].astype(F32)
    for i in range(1, 16):
        total = total + got_ref[i].astype(F32)
    piece = total[:24].astype(BF16)
    for i in range(32):
        out_ref[i] = piece
    spare_ref[...] = total[24:].astype(BF16)


def assemble_kernel(got_ref, spare_ref, other_ref, core_ref, conv_ref, short_ref, gain_ref, flat_ref):
    for j in range(8):
        for zl in range(8):
            row = 192 * j + 24 * zl
            flat_ref[row : row + 24] = got_ref[32 * (j // 4) + ZL_ORDER.index(zl) + 8 * (j % 4)].astype(F32)
    for tile in range(TILES - 1):
        for r in range(3):
            value = flat_ref[pl.ds(40 * r + tile, 8, stride=192), :]
            conv_ref[8 * r : 8 * r + 8, 128 * tile : 128 * tile + 128] = value
    halves = [flat_ref[pl.ds(120 + i, 8, stride=192), :] for i in range(2)]
    conv_ref[:, 128 * TILES - 128 :] = jnp.concatenate([halves[0][:, :64], halves[0][:, 64:], halves[1][:, :64]], axis=0)
    gain_ref[...] = jnp.concatenate([halves[1][m : m + 1, 64:] for m in range(3)], axis=1)
    for j in range(8):
        row = 192 * j + 122
        short_ref[24 * j : 24 * j + 24, :128] = flat_ref[row : row + 24]
        short_ref[24 * j : 24 * j + 24, 128:256] = flat_ref[row + 24 : row + 48]
        short_ref[22 * j : 22 * j + 22, 256:] = flat_ref[row + 48 : row + 70]
    mine, other = spare_ref[...].astype(F32), other_ref[...].astype(F32)
    low = core_ref[...] == 0
    short_ref[176:184, 256:] = jnp.where(low, mine, other)
    short_ref[184:, 256:] = jnp.where(low, other, mine)


def forward_kernel(
    before_ref, s_ref, act_ref, ds_ref, w_conv_ref, pos_ref, w_short_ref, gain_ref, spread_ref,
    decoded_ref, grad_latent_ref, z_all,
):
    w_short = w_short_ref[...]
    grad_latent_ref[...] = dot(ds_ref[...], w_short).astype(BF16)
    prev = features(before_ref[...], w_short, gain_ref[...])[-1].astype(F32)
    act = act_ref[...]
    valid = [[(pos_ref[:, t : t + 1] >= 2 - k).astype(F32) for k in range(2)] for t in range(2)]
    taps = [
        jnp.concatenate([prev[:CELLS] * valid[0][0], prev[CELLS:] * valid[1][0]], axis=0).astype(BF16),
        jnp.concatenate([prev[CELLS:] * valid[0][1], act[:CELLS].astype(F32) * valid[1][1]], axis=0).astype(BF16),
        act,
    ]
    for ab in range(9):
        acc = dot(taps[0], w_conv_ref[ab]) + dot(taps[1], w_conv_ref[9 + ab]) + dot(taps[2], w_conv_ref[18 + ab])
        if ab == 4:
            acc = acc + s_ref[...]
        z_all[64 * ab : 64 * ab + 64] = acc.astype(BF16)
    decoded_ref[...] = dot(spread_ref[...], z_all[...]).astype(BF16)


def shape(*dims, dtype=BF16):
    return jax.ShapeDtypeStruct(dims, dtype)


def in_hbm(value):
    return pltpu.with_memory_space_constraint(value, pltpu.HBM)


def call(kernel, name, outs, in_specs, scratch=()):
    return pl.pallas_call(
        kernel,
        out_shape=outs,
        in_specs=in_specs,
        out_specs=jax.tree.map(lambda _: VMEM, outs),
        scratch_shapes=list(scratch),
        compiler_params=pltpu.CompilerParams(vmem_limit_bytes=40 * 1024 * 1024),
        name=name,
    )


VMEM = pl.BlockSpec(memory_space=pltpu.VMEM)
HBM = pl.BlockSpec(memory_space=pltpu.HBM)
ANY = pl.BlockSpec(memory_space=pl.ANY)


def on_device(latent, frame_pos, w_short, gain, w_conv, cotangent):
    lat = latent.reshape(2 * CELLS, C_IN)
    cot = cotangent.reshape(2 * FINE, C)
    gain2 = gain.reshape(1, C)
    w27 = w_conv.reshape(TAPS, C, C)
    w_short_t = jnp.transpose(w_short)
    pool = jnp.asarray(pool_matrix(4), BF16)
    spread = jnp.asarray(pool_matrix(2), BF16)

    tm = ("zl", "y", "c")
    ahead = call(
        ahead_kernel, "ahead_kernel", shape(2 * FINE, C), [HBM, HBM],
        [pltpu.VMEM((1, 2), jnp.int32), pltpu.VMEM((2 * FINE, C), BF16), pltpu.SemaphoreType.DMA((2,))],
    )(in_hbm(frame_pos), in_hbm(cot))
    following = lax.ppermute(ahead, tm, [(i + 1, i) for i in range(63)])
    own, s_val, act, turned_own, pooled, pool_near, conv_near, lat_near, gain_near, pos_near, w_short_near, spread_near = call(
        own_kernel, "own_kernel",
        [
            shape(8, SEND_ROWS, 128), shape(2 * CELLS, C, dtype=F32), shape(2 * CELLS, C), shape(2, 128, C, dtype=F32),
            shape(2 * CELLS, C, dtype=F32), shape(4 * FINE, 9 * 128), shape(TAPS, C, C),
            shape(2 * CELLS, C_IN), shape(1, C, dtype=F32), shape(1, 2, dtype=jnp.int32),
            shape(C, C_IN), shape(2 * FINE, 18 * CELLS),
        ],
        [HBM] * 8,
        [pltpu.VMEM((2 * FINE, C), BF16), pltpu.VMEM((2, C, 128), F32), pltpu.SemaphoreType.DMA((8,))],
    )(*map(in_hbm, (lat, w_short_t, gain2, cot, frame_pos, pool, w27, spread)))
    send, ds_flat = call(
        local_kernel, "local_kernel", [shape(8, SEND_ROWS, 128), shape(2 * CELLS, C)],
        [VMEM] * 10, [pltpu.VMEM((2, C, 128), F32)],
    )(following, own, s_val, turned_own, pooled, pool_near, conv_near, lat_near, gain_near, pos_near)
    got = lax.all_to_all(send, ("c", "y"), 0, 0)
    part = call(
        kernel_grad_kernel, "kernel_grad_kernel", shape(4, MSG, 128), [VMEM, VMEM],
        [
            pltpu.VMEM((120, 1024), F32), pltpu.VMEM((96, 1024), F32),
            pltpu.VMEM((6, 1024, 256), BF16), pltpu.VMEM((1024, 128), F32),
        ],
    )(got, pool_near)
    got = lax.all_to_all(part, "x", 0, 0)
    part = call(sum_x_kernel, "sum_x_kernel", shape(16, 32, 128), [VMEM])(got)
    got = lax.all_to_all(part, ("zh", "zl"), 0, 0, axis_index_groups=[[(Z_FIRST + i) % 16 for i in range(16)]])
    part, spare, lat_late = call(
        sum_z_kernel, "sum_z_kernel", [shape(32, 24, 128), shape(8, 128), shape(2 * CELLS, C_IN)], [VMEM, VMEM]
    )(got, lat_near)
    before = lax.ppermute(lat_late, tm, [(i, i + 1) for i in range(63)])
    decoded, grad_latent = call(
        forward_kernel, "forward_kernel", [shape(2 * FINE, C), shape(2 * CELLS, C_IN)],
        [VMEM] * 9, [pltpu.VMEM((9 * 2 * CELLS, C), BF16)],
    )(before, s_val, act, ds_flat, conv_near, pos_near, w_short_near, gain_near, spread_near)
    got = lax.all_to_all(part, ("zl", "y"), 0, 0, axis_index_groups=[[4 * zl + y for y in range(4) for zl in ZL_ORDER]])
    got = lax.all_gather(got, "c", axis=0, tiled=True)
    spare_other = lax.ppermute(spare, "c", [(0, 1), (1, 0)])
    grad_conv, grad_short_t, grad_gain = call(
        assemble_kernel, "assemble_kernel",
        [shape(24, TAPS * C, dtype=F32), shape(C, C_IN, dtype=F32), shape(1, C, dtype=F32)],
        [VMEM] * 4, [pltpu.VMEM((1536, 128), F32)],
    )(got, spare, spare_other, lax.axis_index("c").astype(jnp.int32).reshape(1, 1))
    return (
        decoded.reshape(cotangent.shape),
        grad_latent.reshape(latent.shape),
        grad_conv,
        jnp.transpose(grad_short_t),
        grad_gain.reshape(C),
    )


def solution(mesh):
    fine = Mesh(mesh.devices.reshape(8, 4, 2, 4, 2), ("zl", "y", "c", "x", "zh"))
    tm, dp = ("zl", "y", "c"), ("x", "zh")
    return jax.shard_map(
        on_device,
        mesh=fine,
        in_specs=(
            P(dp, tm, None, None, None),
            P(dp, tm),
            P(),
            P(),
            P(),
            P(dp, tm, None, None, None),
        ),
        out_specs=(
            P(dp, tm, None, None, None),
            P(dp, tm, None, None, None),
            P(dp, None),
            P(),
            P(),
        ),
        check_vma=False,
    )
```

```python
import jax
import jax.numpy as jnp
import numpy as np
from jax import lax
from jax.experimental import pallas as pl
from jax.experimental.pallas import tpu as pltpu
from jax.sharding import Mesh, PartitionSpec as P

EPS = 1e-06
C_IN = 384
C = 192
CELLS = 32
FINE = 128
TAPS = 27
Z_FIRST = 10
ZL_ORDER = (4, 3, 5, 2, 6, 1, 7, 0)
TILES = 41
SHORT_ROWS = 80
SEND_ROWS = 192 + SHORT_ROWS
MSG = 256 + SHORT_ROWS
BF16 = jnp.bfloat16
F32 = jnp.float32


def pool_matrix(frames):
    out = np.zeros((frames, 8, 16, 3, 3, frames, 4, 8), np.float32)
    for t in range(frames):
        for a in range(3):
            for b in range(3):
                for p in range(8):
                    for q in range(16):
                        row, col = p + a - 1, q + b - 1
                        if 0 <= row < 8 and 0 <= col < 16:
                            out[t, p, q, a, b, t, row // 2, col // 2] = 1
    return out.reshape(frames * FINE, 9 * frames * CELLS)


def dot(a, b):
    return jnp.dot(a, b, preferred_element_type=F32)


def dot_nt(a, b):
    return lax.dot_general(a, b, (((1,), (1,)), ((), ())), preferred_element_type=F32)


def activation(s_val, gain):
    scale = lax.rsqrt(jnp.mean(s_val * s_val, axis=-1, keepdims=True) + EPS)
    normed = s_val * scale
    z_val = normed * gain
    return scale, normed, z_val, 1.0 / (1.0 + jnp.exp(-z_val))


def features(inputs, w_short_t, gain):
    s_val = dot_nt(inputs, w_short_t)
    _, _, z_val, sig = activation(s_val, gain)
    return s_val, (z_val * sig).astype(BF16)


def start_loads(pairs, sems):
    loads = [pltpu.make_async_copy(source, target, sems.at[i]) for i, (source, target) in enumerate(pairs)]
    for load in loads:
        load.start()
    return loads


def slices_for(turned_ref, tiles, j):
    return jnp.concatenate(
        [turned_ref[t, pl.ds(8 * r + j, 8, stride=24), :] for t in tiles for r in range(3)], axis=0
    ).astype(BF16)


def ahead_kernel(pos_hbm, cot_hbm, ahead_ref, pos_ref, cot_ref, sems):
    for load in start_loads([(pos_hbm, pos_ref), (cot_hbm, cot_ref)], sems):
        load.wait()
    keep = [(pos_ref[:, t : t + 1] >= t + 1).astype(F32) for t in range(2)]
    for t in range(2):
        rows = slice(FINE * t, FINE * t + FINE)
        ahead_ref[rows] = (cot_ref[rows].astype(F32) * keep[t]).astype(BF16)


def two_taps(w_conv_ref, k, ab):
    return jnp.concatenate([w_conv_ref[9 * k + ab], w_conv_ref[9 * k + 9 + ab]], axis=0)


def own_kernel(
    lat_hbm, w_short_hbm, gain_hbm, cot_hbm, pos_hbm, pool_hbm, w_conv_hbm, spread_hbm,
    send_ref, s_ref, act_ref, turned_own_ref, pooled_ref, pool_ref, w_conv_ref, lat_ref, gain_ref, pos_ref,
    w_short_ref, spread_ref, cot_ref, turned_ref, sems,
):
    loads = start_loads([
        (lat_hbm, lat_ref), (w_short_hbm, w_short_ref), (gain_hbm, gain_ref), (cot_hbm, cot_ref),
        (pool_hbm, pool_ref), (w_conv_hbm, w_conv_ref), (pos_hbm, pos_ref),
        (spread_hbm, spread_ref),
    ], sems)
    loads[3].wait()
    fine_t = jnp.transpose(cot_ref[...].astype(F32))
    for t in range(2):
        turned_ref[t, :C] = fine_t[:, 128 * t : 128 * t + 128]
    for load in loads[:3]:
        load.wait()
    s_val, act = features(lat_ref[...], w_short_ref[...], gain_ref[...])
    s_ref[...] = s_val
    act_ref[...] = act
    tail = jnp.concatenate([act[:CELLS, 128:], act[CELLS:, 128:]], axis=1)
    packed = jnp.concatenate([act[:, :128], tail], axis=0)

    for j in range(8):
        send_ref[j, :48] = slices_for(turned_ref, (0, 1), j)
        send_ref[j, 96:192] = packed

    fine_t = fine_t.astype(BF16)
    loads[4].wait()
    loads[5].wait()
    acc = None
    for ab in range(9):
        part = dot(fine_t, pool_ref[: 2 * FINE, ab * 128 : (ab + 1) * 128])
        if ab == 4:
            pooled_ref[...] = jnp.transpose(part)[: 2 * CELLS]
        value = dot(two_taps(w_conv_ref, 1, ab), part.astype(BF16))
        acc = value if acc is None else acc + value
    for i in range(2):
        turned_own_ref[i] = jnp.transpose(acc[C * i : C * i + C])
    loads[6].wait()
    loads[7].wait()


def local_kernel(
    next_ref, sent_ref, s_ref, turned_own_ref, pooled_ref, pool_ref, w_conv_ref, lat_ref, gain_ref, pos_ref,
    send_ref, ds_ref, turned_ref,
):
    fine_t = jnp.transpose(next_ref[...].astype(F32))
    for t in range(2):
        turned_ref[t, :C] = fine_t[:, 128 * t : 128 * t + 128]
    for j in range(8):
        send_ref[j, :48] = sent_ref[j, :48]
        send_ref[j, 48:96] = slices_for(turned_ref, (0, 1), j)
        send_ref[j, 96:192] = sent_ref[j, 96:192]

    fine_t = fine_t.astype(BF16)
    acc = None
    for ab in range(9):
        part = dot(fine_t, pool_ref[2 * FINE :, ab * 128 : (ab + 1) * 128])
        value = dot(two_taps(w_conv_ref, 0, ab), part.astype(BF16))
        acc = value if acc is None else acc + value
    after = [jnp.transpose(acc[C * i : C * i + C]) for i in range(2)]
    tap1, tap2 = turned_own_ref[0], turned_own_ref[1]
    follows = (pos_ref[:, 1:] >= 1).astype(F32)
    gain = gain_ref[...]
    early = tap2[:32] + follows * (tap1[32:64] + after[0][64:96])
    late = tap2[32:64] + after[1][64:96] + after[0][96:]
    grad_act = jnp.concatenate([early, late], axis=0)
    scale, normed, z_val, sig = activation(s_ref[...], gain)
    dz_val = grad_act * sig * (1.0 + z_val * (1.0 - sig))
    gain_term = jnp.sum(dz_val * normed, axis=0, keepdims=True)
    dn_val = dz_val * gain
    ds_val = scale * (dn_val - normed * jnp.mean(dn_val * normed, axis=-1, keepdims=True)) + pooled_ref[...]
    ds_ref[...] = ds_val.astype(BF16)

    short_t = dot(jnp.transpose(ds_val).astype(BF16), lat_ref[...])
    flag = jnp.broadcast_to(follows, (1, 128))
    for j in range(8):
        piece = gain_term[:, 64 * (j % 3) : 64 * (j % 3) + 64]
        spare = 176 + 8 * (j // 4)
        flat = jnp.concatenate([
            short_t[24 * j : 24 * j + 24, :128], short_t[24 * j : 24 * j + 24, 128:256],
            short_t[22 * j : 22 * j + 22, 256:], short_t[spare : spare + 8, 256:],
            jnp.concatenate([piece, piece], axis=1), flag,
        ], axis=0)
        send_ref[j, 192:] = flat.astype(BF16)


def kernel_grad_kernel(got_ref, pool_ref, out_ref, even_ref, odd_ref, rhs_ref, flat_ref):
    none = jnp.zeros((CELLS, C), F32)
    gap = jnp.zeros((4 * CELLS, 64), F32)
    peers = []
    short = jnp.zeros((SHORT_ROWS, 128), F32)
    for p in range(8):
        block = got_ref[p, :96].astype(F32)
        peers.append(jnp.concatenate([block[24 * i : 24 * i + 24] for i in range(4)], axis=1))
        tail = got_ref[p, 160:192].astype(F32)
        act = jnp.concatenate(
            [got_ref[p, 96:160].astype(F32), jnp.concatenate([tail[:, :64], tail[:, 64:]], axis=0)], axis=1)
        extra = got_ref[p, 192:].astype(F32)
        short = short + extra
        act0, act1 = act[:CELLS], act[CELLS:]
        mine = act0 * extra[79:80, :1]
        rows = [[none, none, mine, act1], [none, mine, act1, none], [act0, act1, none, none]]
        for k in range(3):
            value = jnp.concatenate(rows[k], axis=0)
            rhs_ref[2 * k, 128 * p : 128 * p + 128] = jnp.concatenate([value, gap], axis=1).astype(BF16)
            rhs_ref[2 * k + 1, 128 * p : 128 * p + 128] = jnp.concatenate([gap, value], axis=1).astype(BF16)
    fine_t = jnp.concatenate(peers, axis=0).astype(BF16)
    for ab in range(9):
        part = dot(fine_t, pool_ref[:, ab * 128 : (ab + 1) * 128])
        wide = jnp.concatenate([part[24 * p : 24 * p + 24] for p in range(8)], axis=1)
        target = odd_ref if ab % 2 else even_ref
        target[24 * (ab // 2) : 24 * (ab // 2) + 24] = wide
    flat_ref[...] = jnp.zeros(flat_ref.shape, F32)
    lhs = [even_ref[...].astype(BF16), odd_ref[...].astype(BF16)]
    found = {}
    for k in range(3):
        for parity in range(2):
            value = dot(lhs[parity], rhs_ref[2 * k + (9 * k + parity) % 2])
            for i in range(5 - parity):
                found[9 * k + 2 * i + parity] = value[24 * i : 24 * i + 24]

    def place(tile, value):
        for r in range(3):
            flat_ref[pl.ds(40 * r + tile, 8, stride=128), :] = value[8 * r : 8 * r + 8]

    for n in range(0, TAPS, 2):
        tile = 3 * (n // 2)
        place(tile, found[n][:, :128])
        if n + 1 < TAPS:
            place(tile + 1, found[n][:, 128:] + found[n + 1][:, :128])
            place(tile + 2, found[n + 1][:, 128:])
        else:
            half = found[n][:, 128:192]
            gain_piece = jnp.broadcast_to(short[78:79, 64:], (8, 64))
            flat_ref[pl.ds(120, 8, stride=128), :] = jnp.concatenate([half[:8], half[8:16]], axis=1)
            flat_ref[pl.ds(121, 8, stride=128), :] = jnp.concatenate([half[16:], gain_piece], axis=1)
    short = short.astype(BF16)
    for x in range(4):
        out_ref[x, :256] = flat_ref[256 * x : 256 * x + 256].astype(BF16)
        out_ref[x, 256:] = short


def sum_x_kernel(got_ref, out_ref):
    total = got_ref[0].astype(F32)
    for i in range(1, 4):
        total = total + got_ref[i].astype(F32)
    for zh in range(2):
        chunks = jnp.concatenate([total[128 * zh : 128 * zh + 122], total[256:326]], axis=0)
        for zl in range(8):
            piece = jnp.concatenate([chunks[24 * zl : 24 * zl + 24], total[326:334]], axis=0)
            out_ref[(8 * zh + zl - Z_FIRST) % 16] = piece.astype(BF16)


def sum_z_kernel(got_ref, lat_ref, out_ref, spare_ref, lat_out_ref):
    lat_out_ref[...] = lat_ref[...]
    total = got_ref[0].astype(F32)
    for i in range(1, 16):
        total = total + got_ref[i].astype(F32)
    piece = total[:24].astype(BF16)
    for i in range(32):
        out_ref[i] = piece
    spare_ref[...] = total[24:].astype(BF16)


def assemble_kernel(got_ref, spare_ref, other_ref, core_ref, conv_ref, short_ref, gain_ref, flat_ref):
    for j in range(8):
        for zl in range(8):
            row = 192 * j + 24 * zl
            flat_ref[row : row + 24] = got_ref[32 * (j // 4) + ZL_ORDER.index(zl) + 8 * (j % 4)].astype(F32)
    for tile in range(TILES - 1):
        for r in range(3):
            value = flat_ref[pl.ds(40 * r + tile, 8, stride=192), :]
            conv_ref[8 * r : 8 * r + 8, 128 * tile : 128 * tile + 128] = value
    halves = [flat_ref[pl.ds(120 + i, 8, stride=192), :] for i in range(2)]
    conv_ref[:, 128 * TILES - 128 :] = jnp.concatenate([halves[0][:, :64], halves[0][:, 64:], halves[1][:, :64]], axis=0)
    gain_ref[...] = jnp.concatenate([halves[1][m : m + 1, 64:] for m in range(3)], axis=1)
    for j in range(8):
        row = 192 * j + 122
        short_ref[24 * j : 24 * j + 24, :128] = flat_ref[row : row + 24]
        short_ref[24 * j : 24 * j + 24, 128:256] = flat_ref[row + 24 : row + 48]
        short_ref[22 * j : 22 * j + 22, 256:] = flat_ref[row + 48 : row + 70]
    mine, other = spare_ref[...].astype(F32), other_ref[...].astype(F32)
    low = core_ref[...] == 0
    short_ref[176:184, 256:] = jnp.where(low, mine, other)
    short_ref[184:, 256:] = jnp.where(low, other, mine)


def forward_kernel(
    before_ref, s_ref, act_ref, ds_ref, w_conv_ref, pos_ref, w_short_ref, gain_ref, spread_ref,
    decoded_ref, grad_latent_ref, z_all,
):
    w_short = w_short_ref[...]
    grad_latent_ref[...] = dot(ds_ref[...], w_short).astype(BF16)
    prev = features(before_ref[...], w_short, gain_ref[...])[-1].astype(F32)
    act = act_ref[...]
    valid = [[(pos_ref[:, t : t + 1] >= 2 - k).astype(F32) for k in range(2)] for t in range(2)]
    taps = [
        jnp.concatenate([prev[:CELLS] * valid[0][0], prev[CELLS:] * valid[1][0]], axis=0).astype(BF16),
        jnp.concatenate([prev[CELLS:] * valid[0][1], act[:CELLS].astype(F32) * valid[1][1]], axis=0).astype(BF16),
        act,
    ]
    for ab in range(9):
        acc = dot(taps[0], w_conv_ref[ab]) + dot(taps[1], w_conv_ref[9 + ab]) + dot(taps[2], w_conv_ref[18 + ab])
        if ab == 4:
            acc = acc + s_ref[...]
        z_all[64 * ab : 64 * ab + 64] = acc.astype(BF16)
    decoded_ref[...] = dot(spread_ref[...], z_all[...]).astype(BF16)


def shape(*dims, dtype=BF16):
    return jax.ShapeDtypeStruct(dims, dtype)


def in_hbm(value):
    return pltpu.with_memory_space_constraint(value, pltpu.HBM)


def call(kernel, name, outs, in_specs, scratch=()):
    return pl.pallas_call(
        kernel,
        out_shape=outs,
        in_specs=in_specs,
        out_specs=jax.tree.map(lambda _: VMEM, outs),
        scratch_shapes=list(scratch),
        compiler_params=pltpu.CompilerParams(vmem_limit_bytes=40 * 1024 * 1024),
        name=name,
    )


VMEM = pl.BlockSpec(memory_space=pltpu.VMEM)
HBM = pl.BlockSpec(memory_space=pltpu.HBM)
ANY = pl.BlockSpec(memory_space=pl.ANY)


def on_device(latent, frame_pos, w_short, gain, w_conv, cotangent):
    lat = latent.reshape(2 * CELLS, C_IN)
    cot = cotangent.reshape(2 * FINE, C)
    gain2 = gain.reshape(1, C)
    w27 = w_conv.reshape(TAPS, C, C)
    w_short_t = jnp.transpose(w_short)
    pool = jnp.asarray(pool_matrix(4), BF16)
    spread = jnp.asarray(pool_matrix(2), BF16)

    tm = ("zl", "y", "c")
    ahead = call(
        ahead_kernel, "ahead_kernel", shape(2 * FINE, C), [HBM, HBM],
        [pltpu.VMEM((1, 2), jnp.int32), pltpu.VMEM((2 * FINE, C), BF16), pltpu.SemaphoreType.DMA((2,))],
    )(in_hbm(frame_pos), in_hbm(cot))
    following = lax.ppermute(ahead, tm, [(i + 1, i) for i in range(63)])
    own, s_val, act, turned_own, pooled, pool_near, conv_near, lat_near, gain_near, pos_near, w_short_near, spread_near = call(
        own_kernel, "own_kernel",
        [
            shape(8, SEND_ROWS, 128), shape(2 * CELLS, C, dtype=F32), shape(2 * CELLS, C), shape(2, 128, C, dtype=F32),
            shape(2 * CELLS, C, dtype=F32), shape(4 * FINE, 9 * 128), shape(TAPS, C, C),
            shape(2 * CELLS, C_IN), shape(1, C, dtype=F32), shape(1, 2, dtype=jnp.int32),
            shape(C, C_IN), shape(2 * FINE, 18 * CELLS),
        ],
        [HBM] * 8,
        [pltpu.VMEM((2 * FINE, C), BF16), pltpu.VMEM((2, C + 24, 128), F32), pltpu.SemaphoreType.DMA((8,))],
    )(*map(in_hbm, (lat, w_short_t, gain2, cot, frame_pos, pool, w27, spread)))
    send, ds_flat = call(
        local_kernel, "local_kernel", [shape(8, SEND_ROWS, 128), shape(2 * CELLS, C)],
        [VMEM] * 10, [pltpu.VMEM((2, C + 24, 128), F32)],
    )(following, own, s_val, turned_own, pooled, pool_near, conv_near, lat_near, gain_near, pos_near)
    got = lax.all_to_all(send, ("c", "y"), 0, 0)
    part = call(
        kernel_grad_kernel, "kernel_grad_kernel", shape(4, MSG, 128), [VMEM, VMEM],
        [
            pltpu.VMEM((120, 1024), F32), pltpu.VMEM((96, 1024), F32),
            pltpu.VMEM((6, 1024, 256), BF16), pltpu.VMEM((1152, 128), F32),
        ],
    )(got, pool_near)
    got = lax.all_to_all(part, "x", 0, 0)
    part = call(sum_x_kernel, "sum_x_kernel", shape(16, 32, 128), [VMEM])(got)
    got = lax.all_to_all(part, ("zh", "zl"), 0, 0, axis_index_groups=[[(Z_FIRST + i) % 16 for i in range(16)]])
    part, spare, lat_late = call(
        sum_z_kernel, "sum_z_kernel", [shape(32, 24, 128), shape(8, 128), shape(2 * CELLS, C_IN)], [VMEM, VMEM]
    )(got, lat_near)
    before = lax.ppermute(lat_late, tm, [(i, i + 1) for i in range(63)])
    decoded, grad_latent = call(
        forward_kernel, "forward_kernel", [shape(2 * FINE, C), shape(2 * CELLS, C_IN)],
        [VMEM] * 9, [pltpu.VMEM((9 * 2 * CELLS, C), BF16)],
    )(before, s_val, act, ds_flat, conv_near, pos_near, w_short_near, gain_near, spread_near)
    got = lax.all_to_all(part, ("zl", "y"), 0, 0, axis_index_groups=[[4 * zl + y for y in range(4) for zl in ZL_ORDER]])
    got = lax.all_gather(got, "c", axis=0, tiled=True)
    spare_other = lax.ppermute(spare, "c", [(0, 1), (1, 0)])
    grad_conv, grad_short_t, grad_gain = call(
        assemble_kernel, "assemble_kernel",
        [shape(24, TAPS * C, dtype=F32), shape(C, C_IN, dtype=F32), shape(1, C, dtype=F32)],
        [VMEM] * 4, [pltpu.VMEM((1664, 128), F32)],
    )(got, spare, spare_other, lax.axis_index("c").astype(jnp.int32).reshape(1, 1))
    return (
        decoded.reshape(cotangent.shape),
        grad_latent.reshape(latent.shape),
        grad_conv,
        jnp.transpose(grad_short_t),
        grad_gain.reshape(C),
    )


def solution(mesh):
    fine = Mesh(mesh.devices.reshape(8, 4, 2, 4, 2), ("zl", "y", "c", "x", "zh"))
    tm, dp = ("zl", "y", "c"), ("x", "zh")
    return jax.shard_map(
        on_device,
        mesh=fine,
        in_specs=(
            P(dp, tm, None, None, None),
            P(dp, tm),
            P(),
            P(),
            P(),
            P(dp, tm, None, None, None),
        ),
        out_specs=(
            P(dp, tm, None, None, None),
            P(dp, tm, None, None, None),
            P(dp, None),
            P(),
            P(),
        ),
        check_vma=False,
    )
```

```python
import jax
import jax.numpy as jnp
import numpy as np
from jax import lax
from jax.experimental import pallas as pl
from jax.experimental.pallas import tpu as pltpu
from jax.sharding import Mesh, PartitionSpec as P

EPS = 1e-06
C_IN = 384
C = 192
CELLS = 32
FINE = 128
TAPS = 27
Z_FIRST = 10
ZL_ORDER = (4, 3, 5, 2, 6, 1, 7, 0)
TILES = 41
SHORT_ROWS = 80
SEND_ROWS = 192 + SHORT_ROWS
MSG = 256 + SHORT_ROWS
BF16 = jnp.bfloat16
F32 = jnp.float32


def pool_matrix(frames):
    out = np.zeros((frames, 8, 16, 3, 3, frames, 4, 8), np.float32)
    for t in range(frames):
        for a in range(3):
            for b in range(3):
                for p in range(8):
                    for q in range(16):
                        row, col = p + a - 1, q + b - 1
                        if 0 <= row < 8 and 0 <= col < 16:
                            out[t, p, q, a, b, t, row // 2, col // 2] = 1
    return out.reshape(frames * FINE, 9 * frames * CELLS)


def dot(a, b):
    return jnp.dot(a, b, preferred_element_type=F32)


def dot_nt(a, b):
    return lax.dot_general(a, b, (((1,), (1,)), ((), ())), preferred_element_type=F32)


def activation(s_val, gain):
    scale = lax.rsqrt(jnp.mean(s_val * s_val, axis=-1, keepdims=True) + EPS)
    normed = s_val * scale
    z_val = normed * gain
    return scale, normed, z_val, 1.0 / (1.0 + jnp.exp(-z_val))


def features(inputs, w_short_t, gain):
    s_val = dot_nt(inputs, w_short_t)
    _, _, z_val, sig = activation(s_val, gain)
    return s_val, (z_val * sig).astype(BF16)


def start_loads(pairs, sems):
    loads = [pltpu.make_async_copy(source, target, sems.at[i]) for i, (source, target) in enumerate(pairs)]
    for load in loads:
        load.start()
    return loads


def slices_for(turned_ref, tiles, j):
    return jnp.concatenate(
        [turned_ref[t, pl.ds(8 * r + j, 8, stride=24), :] for t in tiles for r in range(3)], axis=0
    ).astype(BF16)


def ahead_kernel(pos_hbm, cot_hbm, ahead_ref, pos_ref, cot_ref, sems):
    for load in start_loads([(pos_hbm, pos_ref), (cot_hbm, cot_ref)], sems):
        load.wait()
    keep = [(pos_ref[:, t : t + 1] >= t + 1).astype(F32) for t in range(2)]
    for t in range(2):
        rows = slice(FINE * t, FINE * t + FINE)
        ahead_ref[rows] = (cot_ref[rows].astype(F32) * keep[t]).astype(BF16)


def pooled_parts(fine_t, pool_ref, rows):
    parts = []
    for start in range(0, 9 * 128, 256):
        wide = dot(fine_t, pool_ref[rows, start : min(start + 256, 9 * 128)])
        parts += [wide[:, i : i + 128] for i in range(0, wide.shape[1], 128)]
    return parts


def two_taps(w_conv_ref, k, ab):
    return jnp.concatenate([w_conv_ref[9 * k + ab], w_conv_ref[9 * k + 9 + ab]], axis=0)


def own_kernel(
    lat_hbm, w_short_hbm, gain_hbm, cot_hbm, pos_hbm, pool_hbm, w_conv_hbm, spread_hbm,
    send_ref, s_ref, act_ref, turned_own_ref, pooled_ref, pool_ref, w_conv_ref, lat_ref, gain_ref, pos_ref,
    w_short_ref, spread_ref, cot_ref, turned_ref, sems,
):
    loads = start_loads([
        (lat_hbm, lat_ref), (w_short_hbm, w_short_ref), (gain_hbm, gain_ref), (cot_hbm, cot_ref),
        (pool_hbm, pool_ref), (w_conv_hbm, w_conv_ref), (pos_hbm, pos_ref),
        (spread_hbm, spread_ref),
    ], sems)
    loads[3].wait()
    fine_t = jnp.transpose(cot_ref[...].astype(F32))
    for t in range(2):
        turned_ref[t, :C] = fine_t[:, 128 * t : 128 * t + 128]
    for load in loads[:3]:
        load.wait()
    s_val, act = features(lat_ref[...], w_short_ref[...], gain_ref[...])
    s_ref[...] = s_val
    act_ref[...] = act
    tail = jnp.concatenate([act[:CELLS, 128:], act[CELLS:, 128:]], axis=1)
    packed = jnp.concatenate([act[:, :128], tail], axis=0)

    for j in range(8):
        send_ref[j, :48] = slices_for(turned_ref, (0, 1), j)
        send_ref[j, 96:192] = packed

    fine_t = fine_t.astype(BF16)
    loads[4].wait()
    loads[5].wait()
    acc = None
    for ab, part in enumerate(pooled_parts(fine_t, pool_ref, slice(0, 2 * FINE))):
        if ab == 4:
            pooled_ref[...] = jnp.transpose(part)[: 2 * CELLS]
        value = dot(two_taps(w_conv_ref, 1, ab), part.astype(BF16))
        acc = value if acc is None else acc + value
    for i in range(2):
        turned_own_ref[i] = jnp.transpose(acc[C * i : C * i + C])
    loads[6].wait()
    loads[7].wait()


def local_kernel(
    next_ref, sent_ref, s_ref, turned_own_ref, pooled_ref, pool_ref, w_conv_ref, lat_ref, gain_ref, pos_ref,
    send_ref, ds_ref, turned_ref,
):
    fine_t = jnp.transpose(next_ref[...].astype(F32))
    for t in range(2):
        turned_ref[t, :C] = fine_t[:, 128 * t : 128 * t + 128]
    for j in range(8):
        send_ref[j, :48] = sent_ref[j, :48]
        send_ref[j, 48:96] = slices_for(turned_ref, (0, 1), j)
        send_ref[j, 96:192] = sent_ref[j, 96:192]

    fine_t = fine_t.astype(BF16)
    acc = None
    for ab, part in enumerate(pooled_parts(fine_t, pool_ref, slice(2 * FINE, 4 * FINE))):
        value = dot(two_taps(w_conv_ref, 0, ab), part.astype(BF16))
        acc = value if acc is None else acc + value
    after = [jnp.transpose(acc[C * i : C * i + C]) for i in range(2)]
    tap1, tap2 = turned_own_ref[0], turned_own_ref[1]
    follows = (pos_ref[:, 1:] >= 1).astype(F32)
    gain = gain_ref[...]
    early = tap2[:32] + follows * (tap1[32:64] + after[0][64:96])
    late = tap2[32:64] + after[1][64:96] + after[0][96:]
    grad_act = jnp.concatenate([early, late], axis=0)
    scale, normed, z_val, sig = activation(s_ref[...], gain)
    dz_val = grad_act * sig * (1.0 + z_val * (1.0 - sig))
    gain_term = jnp.sum(dz_val * normed, axis=0, keepdims=True)
    dn_val = dz_val * gain
    ds_val = scale * (dn_val - normed * jnp.mean(dn_val * normed, axis=-1, keepdims=True)) + pooled_ref[...]
    ds_ref[...] = ds_val.astype(BF16)

    short_t = dot(jnp.transpose(ds_val).astype(BF16), lat_ref[...])
    flag = jnp.broadcast_to(follows, (1, 128))
    for j in range(8):
        piece = gain_term[:, 64 * (j % 3) : 64 * (j % 3) + 64]
        spare = 176 + 8 * (j // 4)
        flat = jnp.concatenate([
            short_t[24 * j : 24 * j + 24, :128], short_t[24 * j : 24 * j + 24, 128:256],
            short_t[22 * j : 22 * j + 22, 256:], short_t[spare : spare + 8, 256:],
            jnp.concatenate([piece, piece], axis=1), flag,
        ], axis=0)
        send_ref[j, 192:] = flat.astype(BF16)


def kernel_grad_kernel(got_ref, pool_ref, out_ref, even_ref, odd_ref, rhs_ref, flat_ref):
    none = jnp.zeros((CELLS, C), F32)
    gap = jnp.zeros((4 * CELLS, 64), F32)
    peers = []
    short = jnp.zeros((SHORT_ROWS, 128), F32)
    for p in range(8):
        block = got_ref[p, :96].astype(F32)
        peers.append(jnp.concatenate([block[24 * i : 24 * i + 24] for i in range(4)], axis=1))
        tail = got_ref[p, 160:192].astype(F32)
        act = jnp.concatenate(
            [got_ref[p, 96:160].astype(F32), jnp.concatenate([tail[:, :64], tail[:, 64:]], axis=0)], axis=1)
        extra = got_ref[p, 192:].astype(F32)
        short = short + extra
        act0, act1 = act[:CELLS], act[CELLS:]
        mine = act0 * extra[79:80, :1]
        rows = [[none, none, mine, act1], [none, mine, act1, none], [act0, act1, none, none]]
        for k in range(3):
            value = jnp.concatenate(rows[k], axis=0)
            rhs_ref[2 * k, 128 * p : 128 * p + 128] = jnp.concatenate([value, gap], axis=1).astype(BF16)
            rhs_ref[2 * k + 1, 128 * p : 128 * p + 128] = jnp.concatenate([gap, value], axis=1).astype(BF16)
    fine_t = jnp.concatenate(peers, axis=0).astype(BF16)
    for ab, part in enumerate(pooled_parts(fine_t, pool_ref, slice(0, 4 * FINE))):
        wide = jnp.concatenate([part[24 * p : 24 * p + 24] for p in range(8)], axis=1)
        target = odd_ref if ab % 2 else even_ref
        target[24 * (ab // 2) : 24 * (ab // 2) + 24] = wide
    flat_ref[...] = jnp.zeros(flat_ref.shape, F32)
    lhs = [even_ref[...].astype(BF16), odd_ref[...].astype(BF16)]
    found = {}
    for k in range(3):
        for parity in range(2):
            value = dot(lhs[parity], rhs_ref[2 * k + (9 * k + parity) % 2])
            for i in range(5 - parity):
                found[9 * k + 2 * i + parity] = value[24 * i : 24 * i + 24]

    def place(tile, value):
        for r in range(3):
            flat_ref[pl.ds(40 * r + tile, 8, stride=128), :] = value[8 * r : 8 * r + 8]

    for n in range(0, TAPS, 2):
        tile = 3 * (n // 2)
        place(tile, found[n][:, :128])
        if n + 1 < TAPS:
            place(tile + 1, found[n][:, 128:] + found[n + 1][:, :128])
            place(tile + 2, found[n + 1][:, 128:])
        else:
            half = found[n][:, 128:192]
            gain_piece = jnp.broadcast_to(short[78:79, 64:], (8, 64))
            flat_ref[pl.ds(120, 8, stride=128), :] = jnp.concatenate([half[:8], half[8:16]], axis=1)
            flat_ref[pl.ds(121, 8, stride=128), :] = jnp.concatenate([half[16:], gain_piece], axis=1)
    short = short.astype(BF16)
    for x in range(4):
        out_ref[x, :256] = flat_ref[256 * x : 256 * x + 256].astype(BF16)
        out_ref[x, 256:] = short


def sum_x_kernel(got_ref, out_ref):
    total = got_ref[0].astype(F32)
    for i in range(1, 4):
        total = total + got_ref[i].astype(F32)
    for zh in range(2):
        chunks = jnp.concatenate([total[128 * zh : 128 * zh + 122], total[256:326]], axis=0)
        for zl in range(8):
            piece = jnp.concatenate([chunks[24 * zl : 24 * zl + 24], total[326:334]], axis=0)
            out_ref[(8 * zh + zl - Z_FIRST) % 16] = piece.astype(BF16)


def sum_z_kernel(got_ref, lat_ref, out_ref, spare_ref, lat_out_ref):
    lat_out_ref[...] = lat_ref[...]
    total = got_ref[0].astype(F32)
    for i in range(1, 16):
        total = total + got_ref[i].astype(F32)
    piece = total[:24].astype(BF16)
    for i in range(32):
        out_ref[i] = piece
    spare_ref[...] = total[24:].astype(BF16)


def assemble_kernel(got_ref, spare_ref, other_ref, core_ref, conv_ref, short_ref, gain_ref, flat_ref):
    for j in range(8):
        for zl in range(8):
            row = 192 * j + 24 * zl
            flat_ref[row : row + 24] = got_ref[32 * (j // 4) + ZL_ORDER.index(zl) + 8 * (j % 4)].astype(F32)
    for tile in range(TILES - 1):
        for r in range(3):
            value = flat_ref[pl.ds(40 * r + tile, 8, stride=192), :]
            conv_ref[8 * r : 8 * r + 8, 128 * tile : 128 * tile + 128] = value
    halves = [flat_ref[pl.ds(120 + i, 8, stride=192), :] for i in range(2)]
    conv_ref[:, 128 * TILES - 128 :] = jnp.concatenate([halves[0][:, :64], halves[0][:, 64:], halves[1][:, :64]], axis=0)
    gain_ref[...] = jnp.concatenate([halves[1][m : m + 1, 64:] for m in range(3)], axis=1)
    for j in range(8):
        row = 192 * j + 122
        short_ref[24 * j : 24 * j + 24, :128] = flat_ref[row : row + 24]
        short_ref[24 * j : 24 * j + 24, 128:256] = flat_ref[row + 24 : row + 48]
        short_ref[22 * j : 22 * j + 22, 256:] = flat_ref[row + 48 : row + 70]
    mine, other = spare_ref[...].astype(F32), other_ref[...].astype(F32)
    low = core_ref[...] == 0
    short_ref[176:184, 256:] = jnp.where(low, mine, other)
    short_ref[184:, 256:] = jnp.where(low, other, mine)


def forward_kernel(
    before_ref, s_ref, act_ref, ds_ref, w_conv_ref, pos_ref, w_short_ref, gain_ref, spread_ref,
    decoded_ref, grad_latent_ref, z_all,
):
    w_short = w_short_ref[...]
    grad_latent_ref[...] = dot(ds_ref[...], w_short).astype(BF16)
    prev = features(before_ref[...], w_short, gain_ref[...])[-1].astype(F32)
    act = act_ref[...]
    valid = [[(pos_ref[:, t : t + 1] >= 2 - k).astype(F32) for k in range(2)] for t in range(2)]
    taps = [
        jnp.concatenate([prev[:CELLS] * valid[0][0], prev[CELLS:] * valid[1][0]], axis=0).astype(BF16),
        jnp.concatenate([prev[CELLS:] * valid[0][1], act[:CELLS].astype(F32) * valid[1][1]], axis=0).astype(BF16),
        act,
    ]
    for ab in range(9):
        acc = dot(taps[0], w_conv_ref[ab]) + dot(taps[1], w_conv_ref[9 + ab]) + dot(taps[2], w_conv_ref[18 + ab])
        if ab == 4:
            acc = acc + s_ref[...]
        z_all[64 * ab : 64 * ab + 64] = acc.astype(BF16)
    decoded_ref[...] = dot(spread_ref[...], z_all[...]).astype(BF16)


def shape(*dims, dtype=BF16):
    return jax.ShapeDtypeStruct(dims, dtype)


def in_hbm(value):
    return pltpu.with_memory_space_constraint(value, pltpu.HBM)


def call(kernel, name, outs, in_specs, scratch=()):
    return pl.pallas_call(
        kernel,
        out_shape=outs,
        in_specs=in_specs,
        out_specs=jax.tree.map(lambda _: VMEM, outs),
        scratch_shapes=list(scratch),
        compiler_params=pltpu.CompilerParams(vmem_limit_bytes=40 * 1024 * 1024),
        name=name,
    )


VMEM = pl.BlockSpec(memory_space=pltpu.VMEM)
HBM = pl.BlockSpec(memory_space=pltpu.HBM)
ANY = pl.BlockSpec(memory_space=pl.ANY)


def on_device(latent, frame_pos, w_short, gain, w_conv, cotangent):
    lat = latent.reshape(2 * CELLS, C_IN)
    cot = cotangent.reshape(2 * FINE, C)
    gain2 = gain.reshape(1, C)
    w27 = w_conv.reshape(TAPS, C, C)
    w_short_t = jnp.transpose(w_short)
    pool = jnp.asarray(pool_matrix(4), BF16)
    spread = jnp.asarray(pool_matrix(2), BF16)

    tm = ("zl", "y", "c")
    ahead = call(
        ahead_kernel, "ahead_kernel", shape(2 * FINE, C), [HBM, HBM],
        [pltpu.VMEM((1, 2), jnp.int32), pltpu.VMEM((2 * FINE, C), BF16), pltpu.SemaphoreType.DMA((2,))],
    )(in_hbm(frame_pos), in_hbm(cot))
    following = lax.ppermute(ahead, tm, [(i + 1, i) for i in range(63)])
    own, s_val, act, turned_own, pooled, pool_near, conv_near, lat_near, gain_near, pos_near, w_short_near, spread_near = call(
        own_kernel, "own_kernel",
        [
            shape(8, SEND_ROWS, 128), shape(2 * CELLS, C, dtype=F32), shape(2 * CELLS, C), shape(2, 128, C, dtype=F32),
            shape(2 * CELLS, C, dtype=F32), shape(4 * FINE, 9 * 128), shape(TAPS, C, C),
            shape(2 * CELLS, C_IN), shape(1, C, dtype=F32), shape(1, 2, dtype=jnp.int32),
            shape(C, C_IN), shape(2 * FINE, 18 * CELLS),
        ],
        [HBM] * 8,
        [pltpu.VMEM((2 * FINE, C), BF16), pltpu.VMEM((2, C + 24, 128), F32), pltpu.SemaphoreType.DMA((8,))],
    )(*map(in_hbm, (lat, w_short_t, gain2, cot, frame_pos, pool, w27, spread)))
    send, ds_flat = call(
        local_kernel, "local_kernel", [shape(8, SEND_ROWS, 128), shape(2 * CELLS, C)],
        [VMEM] * 10, [pltpu.VMEM((2, C + 24, 128), F32)],
    )(following, own, s_val, turned_own, pooled, pool_near, conv_near, lat_near, gain_near, pos_near)
    got = lax.all_to_all(send, ("c", "y"), 0, 0)
    part = call(
        kernel_grad_kernel, "kernel_grad_kernel", shape(4, MSG, 128), [VMEM, VMEM],
        [
            pltpu.VMEM((120, 1024), F32), pltpu.VMEM((96, 1024), F32),
            pltpu.VMEM((6, 1024, 256), BF16), pltpu.VMEM((1152, 128), F32),
        ],
    )(got, pool_near)
    got = lax.all_to_all(part, "x", 0, 0)
    part = call(sum_x_kernel, "sum_x_kernel", shape(16, 32, 128), [VMEM])(got)
    got = lax.all_to_all(part, ("zh", "zl"), 0, 0, axis_index_groups=[[(Z_FIRST + i) % 16 for i in range(16)]])
    part, spare, lat_late = call(
        sum_z_kernel, "sum_z_kernel", [shape(32, 24, 128), shape(8, 128), shape(2 * CELLS, C_IN)], [VMEM, VMEM]
    )(got, lat_near)
    before = lax.ppermute(lat_late, tm, [(i, i + 1) for i in range(63)])
    decoded, grad_latent = call(
        forward_kernel, "forward_kernel", [shape(2 * FINE, C), shape(2 * CELLS, C_IN)],
        [VMEM] * 9, [pltpu.VMEM((9 * 2 * CELLS, C), BF16)],
    )(before, s_val, act, ds_flat, conv_near, pos_near, w_short_near, gain_near, spread_near)
    got = lax.all_to_all(part, ("zl", "y"), 0, 0, axis_index_groups=[[4 * zl + y for y in range(4) for zl in ZL_ORDER]])
    got = lax.all_gather(got, "c", axis=0, tiled=True)
    spare_other = lax.ppermute(spare, "c", [(0, 1), (1, 0)])
    grad_conv, grad_short_t, grad_gain = call(
        assemble_kernel, "assemble_kernel",
        [shape(24, TAPS * C, dtype=F32), shape(C, C_IN, dtype=F32), shape(1, C, dtype=F32)],
        [VMEM] * 4, [pltpu.VMEM((1664, 128), F32)],
    )(got, spare, spare_other, lax.axis_index("c").astype(jnp.int32).reshape(1, 1))
    return (
        decoded.reshape(cotangent.shape),
        grad_latent.reshape(latent.shape),
        grad_conv,
        jnp.transpose(grad_short_t),
        grad_gain.reshape(C),
    )


def solution(mesh):
    fine = Mesh(mesh.devices.reshape(8, 4, 2, 4, 2), ("zl", "y", "c", "x", "zh"))
    tm, dp = ("zl", "y", "c"), ("x", "zh")
    return jax.shard_map(
        on_device,
        mesh=fine,
        in_specs=(
            P(dp, tm, None, None, None),
            P(dp, tm),
            P(),
            P(),
            P(),
            P(dp, tm, None, None, None),
        ),
        out_specs=(
            P(dp, tm, None, None, None),
            P(dp, tm, None, None, None),
            P(dp, None),
            P(),
            P(),
        ),
        check_vma=False,
    )
```
